256 devices in a mesh: grp: 4 (over y_lo, core), doc: 16 (over z, y_hi), col: 4 (over x).
Axes of the slice: x: 4, y: 4 (y_hi: 2, y_lo: 2; y = y_hi * 2 + y_lo), z: 8, core: 2. Of those that a mesh axis runs over, the one named last changes fastest.
Arguments:
- mlp_input: bfloat16 [6144, 4096], P('grp', 'col'), may hold values from -6 to 6
- out_grad: bfloat16 [6144, 4096], P('grp', 'col'), may hold values from -6 to 6
- w_gate: bfloat16 [4096, 14336], P('col', 'doc'), may hold values from -0.09375 to 0.09375
- w_up: bfloat16 [4096, 14336], P('col', 'doc'), may hold values from -0.09375 to 0.09375
- w_down: bfloat16 [14336, 4096], P('doc', 'col'), may hold values from -0.046875 to 0.046875
- proj_down_in: bfloat16 [14336, 64], P('doc'), may hold values from -0.046875 to 0.046875
- proj_down_out: bfloat16 [4096, 64], P('col'), may hold values from -0.09375 to 0.09375
- proj_up_in: bfloat16 [4096, 64], P('col'), may hold values from -0.09375 to 0.09375
- proj_up_out: bfloat16 [14336, 64], P('doc'), may hold values from -0.046875 to 0.046875
- store: bfloat16 [32768, 8192], P(('grp', 'doc'), 'col'), may hold values from -100 to 100
- layer_mask: int32 [32768, 2], P(('grp', 'doc')), may hold values 0 or 1
- live_count: int32 [64], P(('grp', 'doc')), may hold values from 1 to 512, 16384 in all
Outputs:
- scores: float32 [24, 32768], P(None, ('grp', 'doc', 'col'))
The draws below stay inside these ranges and needn't reach their ends.
Inputs may be any that keep to these rules, and one draw needn't show every extreme that they name: Owner p = grp index * 16 + doc index holds slots p * 512 to p * 512 + 511; the first live_count[p] of them hold documents.
All inputs are finite; a program needn't handle non-finite values. No bound on the sum of `layer_mask` or of `live_count` on one device may be relied on, other than what follows from the above.
Results may differ from the reference program's by a relative error of at most 0.03.
Values may be sent and summed in bfloat16 or wider, within the bound.
A program may use at most 128 MiB of HBM per device.

```python
import math
import jax
import jax.numpy as jnp
import numpy as np
from jax import lax

D = 4096
FF = 14336
K = 64
SEQ = 256
DOC_DEV = 512
QUERIES = 24
TOKENS = 6144
COLS = 8192
OWNERS = 64
DOCS = 32768
N_COL = 4


def draw_store(key, part):
    key = jax.random.fold_in(key, 11)
    key_rows, key_cols, key_noise = jax.random.split(key, 3)
    row_level = jax.random.uniform(key_rows, (DOCS, 1), jnp.float32)
    col_level = jax.random.uniform(key_cols, (1, COLS), jnp.float32)
    position = jnp.arange(COLS, dtype=jnp.float32)[None, :] / COLS
    base = jnp.clip(jax.random.normal(key_noise, (DOCS, COLS), jnp.float32), -4.0, 4.0)
    trend = 0.5
    scale = jnp.power(10.0, row_level) * jnp.power(10.0, trend * position + 0.5 * col_level)
    return (0.1 * base * scale).astype(jnp.bfloat16)


def touch_ends(values, key, smallest, largest):
    shape = values.shape
    index_at = [jax.random.randint(jax.random.fold_in(key, axis), (), 0, shape[axis]) for axis in range(len(shape))]
    values = values.at[tuple(index_at)].set(smallest)
    longest = shape.index(max(shape))
    index_at[longest] = (index_at[longest] + 1) % shape[longest]
    return values.at[tuple(index_at)].set(largest)


def levels(stream_key, extent, cuts, smallest, high):
    factor_of, own = 1.0, jax.random.fold_in(stream_key, 6)
    for axis_at, blocks in cuts:
        draws = jnp.exp(jax.random.uniform(jax.random.fold_in(own, axis_at), (blocks,), jnp.float32, smallest / len(cuts), high / len(cuts)))
        factor_of = factor_of * jnp.repeat(draws, extent[axis_at] // blocks).reshape([-1 if axis == axis_at else 1 for axis in range(len(extent))])
    return factor_of


def length_profile(count, total, bound, lean):
    weights = [(1 << 20) // math.isqrt(rank ** lean) + 1 for rank in range(2, count + 1)]
    spare, holding = total - bound - (count - 1), [1] * (count - 1)
    while spare > 0:
        candidates = [i for i in range(count - 1) if holding[i] < bound]
        mass, left = sum([weights[i] for i in candidates]), spare
        for i in candidates:
            more = min(bound - holding[i], max(1, left * weights[i] // mass), spare)
            holding[i] = holding[i] + more
            spare = spare - more
    return np.array([bound] + holding)


def uneven(rng, count, total, limit, slope):
    if count == 2:
        one = jax.random.randint(rng, (), max(1, total - limit), min(limit, total - 1) + 1)
        return jnp.stack([one, total - one])
    sizes = jnp.asarray(length_profile(count, total, limit, slope), jnp.int32)
    twos = (count - 1) // 2
    giver, receiver = sizes[1:1 + 2 * twos:2], sizes[2:2 + 2 * twos:2]
    margin = jnp.minimum(giver - 1, limit - receiver)
    moved = jax.random.randint(jax.random.fold_in(rng, 1), (twos,), 0, 1 << 20) % (margin + 1)
    sizes = sizes.at[1:1 + 2 * twos:2].set(giver - moved).at[2:2 + 2 * twos:2].set(receiver + moved)
    return sizes[jax.random.permutation(jax.random.fold_in(rng, 2), count)]


def normal_values(stream_key, shape, deviation, most, shards=(), held_as=jnp.bfloat16):
    level = levels(stream_key, shape, shards, -0.22, 0.18) if shards else 1.0
    values = jax.random.normal(stream_key, shape, jnp.float32) * deviation * level
    return jnp.minimum(jnp.maximum(values, -most), most).astype(held_as)


def setup_inputs(seed: int = 0) -> dict:
    key_of = jax.random.split(jax.random.key(seed), 13)
    mlp_input = normal_values(key_of[0], (TOKENS, D), 1.0, 6.0, ((0, 4), (1, 4)))
    out_grad = normal_values(key_of[1], (TOKENS, D), 1.0, 6.0, ((0, 4), (1, 4)))
    w_gate = normal_values(key_of[2], (D, FF), D ** -0.5, 0.09375, ((0, 4), (1, 16)))
    w_up = normal_values(key_of[3], (D, FF), D ** -0.5, 0.09375, ((0, 4), (1, 16)))
    w_down = normal_values(key_of[4], (FF, D), FF ** -0.5, 0.046875, ((0, 16), (1, 4)))
    proj_down_in = normal_values(key_of[5], (FF, K), FF ** -0.5, 0.046875, ((0, 16),))
    proj_down_out = normal_values(key_of[6], (D, K), D ** -0.5, 0.09375, ((0, 4),))
    proj_up_in = normal_values(key_of[7], (D, K), D ** -0.5, 0.09375, ((0, 4),))
    proj_up_out = normal_values(key_of[8], (FF, K), FF ** -0.5, 0.046875, ((0, 16),))
    store = draw_store(jax.random.fold_in(key_of[12], 71), 0)
    layer_mask = touch_ends((jax.random.randint(key_of[10], (DOCS, 2), 0, 4) < 3).astype(jnp.int32), jax.random.fold_in(key_of[10], 1), 0, 1)
    live_count = uneven(key_of[11], OWNERS, OWNERS * DOC_DEV // 2, DOC_DEV, 2).astype(jnp.int32)
    return dict(mlp_input=mlp_input, out_grad=out_grad, w_gate=w_gate, w_up=w_up, w_down=w_down, proj_down_in=proj_down_in, proj_down_out=proj_down_out, proj_up_in=proj_up_in, proj_up_out=proj_up_out, store=store, layer_mask=layer_mask, live_count=live_count)


epsilon = 1e-06

def rounded_dot(left, right):
    value = jnp.dot(left, right, preferred_element_type=jnp.float32).astype(jnp.bfloat16)
    value = lax.optimization_barrier(value)
    return value.astype(jnp.float32)

def reference(mlp_input, out_grad, w_gate, w_up, w_down, proj_down_in, proj_down_out, proj_up_in, proj_up_out, store, layer_mask, live_count):
    block_width = D // N_COL
    token_count = mlp_input.shape[0]

    def add_block(totals, block_index):
        first = block_index * block_width
        x_part = lax.dynamic_slice_in_dim(mlp_input, first, block_width, 1)
        g_part = lax.dynamic_slice_in_dim(out_grad, first, block_width, 1)
        gate_rows = lax.dynamic_slice_in_dim(w_gate, first, block_width, 0)
        up_rows = lax.dynamic_slice_in_dim(w_up, first, block_width, 0)
        down_cols = lax.dynamic_slice_in_dim(w_down, first, block_width, 1)
        out_rows = lax.dynamic_slice_in_dim(proj_down_out, first, block_width, 0)
        in_rows = lax.dynamic_slice_in_dim(proj_up_in, first, block_width, 0)
        parts = (rounded_dot(x_part, gate_rows), rounded_dot(x_part, up_rows), rounded_dot(g_part, down_cols.T), rounded_dot(g_part, out_rows), rounded_dot(x_part, in_rows))
        return (tuple((total + part for total, part in zip(totals, parts))), None)
    start_sums = (jnp.zeros((token_count, FF), jnp.float32), jnp.zeros((token_count, FF), jnp.float32), jnp.zeros((token_count, FF), jnp.float32), jnp.zeros((token_count, K), jnp.float32), jnp.zeros((token_count, K), jnp.float32))
    sums, unused = lax.scan(add_block, start_sums, jnp.arange(N_COL, dtype=jnp.int32))
    gate_value, up_value, hidden_grad, down_out, up_in = sums
    sigmoid_gate = jax.nn.sigmoid(gate_value)
    hidden = (gate_value * sigmoid_gate * up_value).astype(jnp.bfloat16)
    up_grad = (hidden_grad * gate_value * sigmoid_gate).astype(jnp.bfloat16)
    down_in = jnp.dot(hidden, proj_down_in, preferred_element_type=jnp.float32)
    up_out = jnp.dot(up_grad, proj_up_out, preferred_element_type=jnp.float32)
    down_grads = jnp.einsum('qtk,qtl->qkl', down_out.reshape(QUERIES, SEQ, K), down_in.reshape(QUERIES, SEQ, K), precision=lax.Precision.HIGHEST)
    up_grads = jnp.einsum('qtk,qtl->qkl', up_out.reshape(QUERIES, SEQ, K), up_in.reshape(QUERIES, SEQ, K), precision=lax.Precision.HIGHEST)
    query_grads = jnp.concatenate([down_grads.reshape(QUERIES, K * K), up_grads.reshape(QUERIES, K * K)], axis=1)
    query_norm = jnp.sqrt(lax.optimization_barrier(jnp.mean(query_grads * query_grads, axis=1)) + epsilon)
    query_unit = (query_grads / query_norm[:, None]).astype(jnp.bfloat16)
    module_cols = K * K
    raw_scores = jnp.zeros((QUERIES, DOCS), jnp.float32)
    doc_squares = jnp.zeros((DOCS,), jnp.float32)
    for module in range(2):
        query_part = query_unit[:, module * module_cols:(module + 1) * module_cols]
        store_part = store[:, module * module_cols:(module + 1) * module_cols]
        weight = layer_mask[:, module].astype(jnp.float32)
        raw_scores = raw_scores + weight[None, :] * jnp.dot(query_part, store_part.T, preferred_element_type=jnp.float32)
        doc_squares = doc_squares + weight * lax.optimization_barrier(jnp.sum(jnp.square(store_part.astype(jnp.float32)), axis=1))
    slot_index = jnp.arange(DOCS, dtype=jnp.int32) % DOC_DEV
    live_slots = slot_index < jnp.repeat(live_count, DOC_DEV)
    scaled = raw_scores / (jnp.sqrt(doc_squares / COLS + epsilon) * math.sqrt(COLS))
    return jnp.where(live_slots[None, :], scaled, 0.0)
```

```python
import functools
import math

import jax
import jax.numpy as jnp
from jax import lax
from jax.experimental import pallas as pl
from jax.experimental.pallas import tpu as pltpu
from jax.sharding import PartitionSpec as P

MESH = pl.DeviceIdType.MESH
SEQ = 256
LANES = 128
EPSILON = 1e-06
NT = (((1,), (1,)), ((), ()))
f32, bf16 = jnp.float32, jnp.bfloat16


def dot(left, right):
    return jnp.dot(left, right, preferred_element_type=f32)


def dot_nt(left, right):
    return lax.dot_general(left, right, NT, preferred_element_type=f32)


def kernel(
    sizes,
    x_in,
    og_in,
    wg_in,
    wu_in,
    wd_in,
    pdi_in,
    pdo_in,
    pui_in,
    puo_in,
    store_in,
    mask_in,
    out_ref,
    x,
    og,
    wg,
    wu,
    wd,
    pdi,
    pdo,
    pui,
    puo,
    store,
    mask,
    gate,
    up,
    hg,
    s,
    send_a,
    recv_a,
    send_b,
    recv_b,
    ends_part,
    ends_recv,
    ends,
    ends_t,
    ui2,
    pairs,
    grads,
    x_recv,
    block,
    d_recv,
    full,
    select,
    c_send,
    c_recv,
    load_sem,
    ring_s,
    ring_r,
    ends_s,
    ends_r,
    gather_s,
    gather_r,
    x_s,
    x_r,
    d1_s,
    d1_r,
    d2_s,
    d2_r,
    g_s,
    g_r,
    c_s,
    c_r,
):
    n_grp, n_doc, n_col, nq = sizes
    part = SEQ // n_col
    half = part // 2
    g, d, c = lax.axis_index("grp"), lax.axis_index("doc"), lax.axis_index("col")
    right, left, across = (
        lax.rem(c + 1, n_col),
        lax.rem(c + n_col - 1, n_col),
        lax.rem(c + 2, n_col),
    )

    def remote(src, dst, send, recv, **place):
        return pltpu.make_async_remote_copy(
            src_ref=src,
            dst_ref=dst,
            send_sem=send,
            recv_sem=recv,
            device_id=place,
            device_id_type=MESH,
        )

    loads = {}

    def load(key, src, dst):
        copy = pltpu.make_async_copy(src, dst, load_sem.at[len(loads)])
        copy.start()
        loads[key] = copy

    load("wg", wg_in, wg)
    load("x", x_in, x)
    load("wu", wu_in, wu)
    load("og", og_in, og)
    load("wd", wd_in, wd)
    k_dim = pdi_in.shape[0]
    load("pdo", pdo_in, pdo.at[pl.ds(0, k_dim)])
    load("pui", pui_in, pui.at[pl.ds(k_dim, k_dim)])
    load("pdi", pdi_in, pdi.at[pl.ds(0, k_dim)])
    load("pdi2", pdi_in, pdi.at[pl.ds(k_dim, k_dim)])
    load("puo", puo_in, puo)
    load("store", store_in, store)
    load("mask", mask_in, mask)

    barrier = pltpu.get_barrier_semaphore()
    for k in range(1, n_col):
        pl.semaphore_signal(
            barrier, 1, device_id={"col": lax.rem(c + k, n_col)}, device_id_type=MESH
        )
    for k in range(1, n_grp):
        pl.semaphore_signal(
            barrier, 1, device_id={"grp": lax.rem(g + k, n_grp)}, device_id_type=MESH
        )

    def greet(k, carry):
        pl.semaphore_signal(
            barrier, 1, device_id={"doc": lax.rem(d + k, n_doc)}, device_id_type=MESH
        )
        return carry

    lax.fori_loop(1, n_doc, greet, 0)
    pl.semaphore_wait(barrier, n_col + n_grp + n_doc - 3)

    def copy_a(p, way):
        rows = pl.ds(way * half, half)
        return remote(
            send_a.at[p, rows],
            recv_a.at[p, way],
            ring_s.at[0, p, way],
            ring_r.at[0, p, way],
            col=(right, left)[way],
        )

    def copy_b(p, way):
        return remote(
            send_b.at[p, way],
            recv_b.at[p, way],
            ring_s.at[1, p, way],
            ring_r.at[1, p, way],
            col=(right, left)[way],
        )

    def copy_g(p, way, slot):
        return remote(
            s.at[p, slot],
            s.at[p, slot],
            ring_s.at[2, p, way],
            ring_r.at[2, p, way],
            col=(right, left)[way],
        )

    def copy_f(p, way, slot):
        rows = pl.ds(way * half, half)
        return remote(
            s.at[p, slot, rows],
            s.at[p, slot, rows],
            ring_s.at[3, p, way],
            ring_r.at[3, p, way],
            col=(right, left)[way],
        )

    def token_rows(p):
        return pl.ds(pl.multiple_of(p * SEQ, SEQ), SEQ)

    def own_rows(owner, first, count):
        return pl.ds(pl.multiple_of(owner * part + first, half), count)

    loads["wg"].wait()
    loads["x"].wait()

    def gate_step(p, carry):
        gate[p] = dot(x[token_rows(p)], wg[...])
        send_a[p] = gate[p, own_rows(across, 0, part)].astype(bf16)
        copy_a(p, 0).start()
        copy_a(p, 1).start()
        return carry

    lax.fori_loop(0, nq, gate_step, 0)

    loads["wu"].wait()
    loads["og"].wait()
    loads["wd"].wait()

    def terms_step(p, carry):
        up[p] = dot(x[token_rows(p)], wu[...]).astype(bf16)
        copy_a(p, 0).wait_recv()
        send_b[p, 0, pl.ds(0, half)] = (
            gate[p, own_rows(right, 0, half)] + recv_a[p, 0].astype(f32)
        ).astype(bf16)
        send_b[p, 0, pl.ds(half, half)] = gate[p, own_rows(right, half, half)].astype(bf16)
        copy_b(p, 0).start()
        copy_a(p, 1).wait_recv()
        send_b[p, 1, pl.ds(0, half)] = gate[p, own_rows(left, 0, half)].astype(bf16)
        send_b[p, 1, pl.ds(half, half)] = (
            gate[p, own_rows(left, half, half)] + recv_a[p, 1].astype(f32)
        ).astype(bf16)
        copy_b(p, 1).start()
        hg[p] = dot_nt(og[token_rows(p)], wd[...]).astype(bf16)
        return carry

    lax.fori_loop(0, nq, terms_step, 0)

    slab = ends_part.shape[0]
    loads["pdo"].wait()
    loads["pui"].wait()
    pdo[pl.ds(k_dim, k_dim)] = jnp.zeros((k_dim, pdo.shape[1]), bf16)
    pui[pl.ds(0, k_dim)] = jnp.zeros((k_dim, pui.shape[1]), bf16)
    mine = pl.ds(pl.multiple_of(d * slab, slab), slab)
    ends_part[...] = (dot_nt(og[mine], pdo[...]) + dot_nt(x[mine], pui[...])).astype(bf16)

    def copy_ends(k):
        return remote(
            ends_part,
            ends_recv.at[k - 1],
            ends_s.at[k - 1],
            ends_r.at[k - 1],
            col=lax.rem(c + k, n_col),
        )

    for k in range(1, n_col):
        copy_ends(k).start()

    loads["store"].wait()
    squares = jnp.zeros((store.shape[0], LANES), f32)
    for j in range(store.shape[1] // LANES):
        value = store[:, pl.ds(j * LANES, LANES)].astype(f32)
        squares += value * value
    upper = squares.astype(bf16)
    lower = (squares - upper.astype(f32)).astype(bf16)
    ones = jnp.ones((8, LANES), bf16)
    doc_squares = dot_nt(ones, upper) + dot_nt(ones, lower)
    loads["mask"].wait()
    keep = jnp.where(c < n_col // 2, mask[0:1, :], mask[1:2, :]).astype(f32)
    doc_squares = doc_squares * keep
    out_width = store.shape[0] // n_col
    for j in range(n_col):
        c_send[j, pl.ds(32, 8)] = doc_squares[:, j * out_width : (j + 1) * out_width]

    q_pad = n_doc // 2
    n_pad = q_pad * n_grp
    n_sub = full.shape[0] * full.shape[1] * 8 // n_pad
    row = lax.broadcasted_iota(jnp.int32, (n_pad, n_pad * n_sub), 0)
    lane = lax.broadcasted_iota(jnp.int32, (n_pad, n_pad * n_sub), 1)
    for kk in range(n_sub):
        select[pl.ds(kk * n_pad, n_pad)] = jnp.where(lane == row * n_sub + kk, 1.0, 0.0).astype(
            bf16
        )

    for k in range(1, n_col):
        copy_ends(k).wait_recv()
    total = ends_part[...].astype(f32)
    for k in range(1, n_col):
        total += ends_recv[k - 1].astype(f32)
    ends[mine] = total.astype(bf16)

    def copy_gather(k, owner):
        rows = pl.ds(pl.multiple_of(owner * slab, slab), slab)
        return remote(
            ends.at[rows],
            ends.at[rows],
            gather_s.at[k - 1],
            gather_r.at[k - 1],
            doc=lax.rem(d + k, n_doc),
        )

    def gather_start(k, carry):
        copy_gather(k, d).start()
        return carry

    lax.fori_loop(1, n_doc, gather_start, 0)

    def own_step(p, carry):
        copy_b(p, 0).wait_recv()
        copy_b(p, 1).wait_recv()
        value = (
            gate[p, own_rows(c, 0, part)] + recv_b[p, 0].astype(f32) + recv_b[p, 1].astype(f32)
        )
        s[p, c] = (value * jax.nn.sigmoid(value)).astype(bf16)
        copy_g(p, 0, c).start()
        copy_g(p, 1, c).start()
        return carry

    lax.fori_loop(0, nq, own_step, 0)

    def gather_wait(k, carry):
        copy_gather(k, lax.rem(d + n_doc - k, n_doc)).wait_recv()
        return carry

    lax.fori_loop(1, n_doc, gather_wait, 0)
    low_lanes = lax.broadcasted_iota(jnp.int32, (SEQ, LANES), 1) < k_dim

    def ends_step(p, carry):
        value = ends[token_rows(p)].astype(f32)
        ends_t[p] = value.T[:k_dim].astype(bf16)
        ui2[p] = jnp.where(low_lanes, pltpu.roll(value, k_dim, 1), value).astype(bf16)
        return carry

    lax.fori_loop(0, nq, ends_step, 0)

    def forward_step(p, carry):
        copy_g(p, 0, left).wait_recv()
        copy_f(p, 0, left).start()
        copy_g(p, 1, right).wait_recv()
        copy_f(p, 1, right).start()
        return carry

    lax.fori_loop(0, nq, forward_step, 0)

    loads["pdi"].wait()
    loads["pdi2"].wait()
    loads["puo"].wait()
    for p in range(nq, q_pad):
        grads[p] = jnp.zeros(grads.shape[1:], f32)
    low_half = lax.broadcasted_iota(jnp.int32, (k_dim // 2, LANES), 1) < k_dim

    def grads_step(p, carry):
        copy_f(p, 0, across).wait_recv()
        copy_f(p, 1, across).wait_recv()
        shared = s[p].reshape(SEQ, s.shape[-1])
        down_in = dot_nt(up[p] * shared, pdi[...])
        up_out = dot_nt(puo[...], hg[p] * shared)
        pairs[pl.ds(0, k_dim)] = dot(ends_t[p], down_in.astype(bf16))
        pairs[pl.ds(k_dim, k_dim)] = dot(up_out.astype(bf16), ui2[p])
        for m in range(2):
            even = pairs[pl.ds(m * k_dim, k_dim // 2, 2)]
            odd = pairs[pl.ds(m * k_dim + 1, k_dim // 2, 2)]
            grads[p, pl.ds(m * (k_dim // 2), k_dim // 2)] = jnp.where(low_half, even, odd)
        return carry

    lax.fori_loop(0, nq, grads_step, 0)

    def copy_x(k):
        to = lax.rem(c + k, n_col)
        return remote(
            grads.at[:, pl.ds(pl.multiple_of(to * n_sub, n_sub), n_sub)],
            x_recv.at[k - 1],
            x_s.at[k - 1],
            x_r.at[k - 1],
            col=to,
        )

    for k in range(1, n_col):
        copy_x(k).start()
    for k in range(1, n_col):
        copy_x(k).wait_recv()
    total = grads[:, pl.ds(pl.multiple_of(c * n_sub, n_sub), n_sub)]
    for k in range(1, n_col):
        total += x_recv[k - 1]
    block[...] = total.reshape(block.shape)

    def copy_d1(k):
        to = lax.rem(d + k, n_doc)
        return remote(block.at[to], d_recv.at[k - 1], d1_s.at[k - 1], d1_r.at[k - 1], doc=to)

    def d1_start(k, carry):
        copy_d1(k).start()
        return carry

    lax.fori_loop(1, n_doc, d1_start, 0)

    def d1_wait(k, carry):
        copy_d1(k).wait_recv()
        return carry

    lax.fori_loop(1, n_doc, d1_wait, 0)
    total = block[d]
    for k in range(1, n_doc):
        total += d_recv[k - 1]
    full[g, d] = total

    def copy_d2(k, owner):
        return remote(
            full.at[g, owner],
            full.at[g, owner],
            d2_s.at[k - 1],
            d2_r.at[k - 1],
            doc=lax.rem(d + k, n_doc),
        )

    def d2_start(k, carry):
        copy_d2(k, d).start()
        return carry

    lax.fori_loop(1, n_doc, d2_start, 0)

    def d2_wait(k, carry):
        copy_d2(k, lax.rem(d + n_doc - k, n_doc)).wait_recv()
        return carry

    lax.fori_loop(1, n_doc, d2_wait, 0)

    def copy_grp(k, owner):
        return remote(
            full.at[owner],
            full.at[owner],
            g_s.at[k - 1],
            g_r.at[k - 1],
            grp=lax.rem(g + k, n_grp),
        )

    for k in range(1, n_grp):
        copy_grp(k, g).start()
    for k in range(1, n_grp):
        copy_grp(k, lax.rem(g + n_grp - k, n_grp)).wait_recv()

    ordered = dot(select[...], full[...].reshape(n_pad * n_sub, LANES).astype(bf16))
    query = jnp.concatenate([ordered[kk * n_pad : (kk + 1) * n_pad] for kk in range(n_sub)], axis=1)
    raw = dot_nt(query.astype(bf16), store[...]) * keep
    query_squares = jnp.broadcast_to(
        jnp.sum(query * query, axis=1, keepdims=True), (n_pad, out_width)
    )
    for j in range(n_col):
        c_send[j, pl.ds(0, 32)] = raw[:, j * out_width : (j + 1) * out_width]
        c_send[j, pl.ds(40, 32)] = query_squares

    def copy_c(k):
        to = lax.rem(c + k, n_col)
        return remote(c_send.at[to], c_recv.at[k - 1], c_s.at[k - 1], c_r.at[k - 1], col=to)

    for k in range(1, n_col):
        copy_c(k).start()
    for k in range(1, n_col):
        copy_c(k).wait_recv()
    total = c_send[c]
    for k in range(1, n_col):
        total += c_recv[k - 1]
    columns = float(n_col * n_sub * LANES)
    query_norm = jnp.sqrt(total[40:72] / columns + EPSILON)
    doc_norm = jnp.sqrt(total[32:33] / columns + EPSILON) * math.sqrt(columns)
    out_ref[...] = total[0:32] / (query_norm * doc_norm)

    def ring_done(p, carry):
        for way in range(2):
            copy_a(p, way).wait_send()
            copy_b(p, way).wait_send()
            copy_g(p, way, c).wait_send()
            copy_f(p, way, left).wait_send()
        return carry

    lax.fori_loop(0, nq, ring_done, 0)

    def doc_done(k, carry):
        copy_gather(k, d).wait_send()
        copy_d1(k).wait_send()
        copy_d2(k, d).wait_send()
        return carry

    lax.fori_loop(1, n_doc, doc_done, 0)
    for k in range(1, n_col):
        copy_ends(k).wait_send()
        copy_x(k).wait_send()
        copy_c(k).wait_send()
    for k in range(1, n_grp):
        copy_grp(k, g).wait_send()


def local(
    mlp_input,
    out_grad,
    w_gate,
    w_up,
    w_down,
    proj_down_in,
    proj_down_out,
    proj_up_in,
    proj_up_out,
    store,
    layer_mask,
    live_count,
):
    n_grp, n_doc, n_col = (lax.axis_size(name) for name in ("grp", "doc", "col"))
    tokens, depth = mlp_input.shape
    width = w_gate.shape[1]
    k_dim = proj_down_in.shape[1]
    nq = tokens // SEQ
    q_pad = n_doc // 2
    n_pad = q_pad * n_grp
    part = SEQ // n_col
    slab = tokens // n_doc
    n_row = 2 * k_dim * k_dim // LANES
    n_sub = n_row // n_col
    dma = pltpu.SemaphoreType.DMA
    scratch = [
        pltpu.VMEM((tokens, depth), bf16),
        pltpu.VMEM((tokens, depth), bf16),
        pltpu.VMEM((depth, width), bf16),
        pltpu.VMEM((depth, width), bf16),
        pltpu.VMEM((width, depth), bf16),
        pltpu.VMEM((2 * k_dim, width), bf16),
        pltpu.VMEM((2 * k_dim, depth), bf16),
        pltpu.VMEM((2 * k_dim, depth), bf16),
        pltpu.VMEM((k_dim, width), bf16),
        pltpu.VMEM(store.shape, bf16),
        pltpu.VMEM(layer_mask.shape[::-1], jnp.int32),
        pltpu.VMEM((nq, SEQ, width), f32),
        pltpu.VMEM((nq, SEQ, width), bf16),
        pltpu.VMEM((nq, SEQ, width), bf16),
        pltpu.VMEM((nq, n_col, part, width), bf16),
        pltpu.VMEM((nq, part, width), bf16),
        pltpu.VMEM((nq, 2, part // 2, width), bf16),
        pltpu.VMEM((nq, 2, part, width), bf16),
        pltpu.VMEM((nq, 2, part, width), bf16),
        pltpu.VMEM((slab, LANES), bf16),
        pltpu.VMEM((n_col - 1, slab, LANES), bf16),
        pltpu.VMEM((tokens, LANES), bf16),
        pltpu.VMEM((nq, k_dim, SEQ), bf16),
        pltpu.VMEM((nq, SEQ, LANES), bf16),
        pltpu.VMEM((2 * k_dim, LANES), f32),
        pltpu.VMEM((q_pad, n_row, LANES), f32),
        pltpu.VMEM((n_col - 1, q_pad, n_sub, LANES), f32),
        pltpu.VMEM((n_doc, 8, LANES), f32),
        pltpu.VMEM((n_doc - 1, 8, LANES), f32),
        pltpu.VMEM((n_grp, n_doc, 8, LANES), f32),
        pltpu.VMEM((n_pad * n_sub, n_pad * n_sub), bf16),
        pltpu.VMEM((n_col, 72, store.shape[0] // n_col), f32),
        pltpu.VMEM((n_col - 1, 72, store.shape[0] // n_col), f32),
        dma((12,)),
        dma((4, nq, 2)),
        dma((4, nq, 2)),
        dma((n_col - 1,)),
        dma((n_col - 1,)),
        dma((n_doc - 1,)),
        dma((n_doc - 1,)),
        dma((n_col - 1,)),
        dma((n_col - 1,)),
        dma((n_doc - 1,)),
        dma((n_doc - 1,)),
        dma((n_doc - 1,)),
        dma((n_doc - 1,)),
        dma((n_grp - 1,)),
        dma((n_grp - 1,)),
        dma((n_col - 1,)),
        dma((n_col - 1,)),
    ]
    out_width = store.shape[0] // n_col
    scores = pl.pallas_call(
        functools.partial(kernel, (n_grp, n_doc, n_col, nq)),
        out_shape=jax.ShapeDtypeStruct((n_pad, out_width), f32),
        in_specs=[pl.BlockSpec(memory_space=pl.ANY)] * 11,
        out_specs=pl.BlockSpec(memory_space=pltpu.VMEM),
        scratch_shapes=scratch,
        compiler_params=pltpu.CompilerParams(
            collective_id=0, has_side_effects=True, vmem_limit_bytes=58 * 1024 * 1024
        ),
        cost_estimate=pl.CostEstimate(
            flops=6 * tokens * depth * width, bytes_accessed=14 << 20, transcendentals=0
        ),
    )(
        mlp_input,
        out_grad,
        w_gate,
        w_up,
        w_down,
        proj_down_in.T,
        proj_down_out.T,
        proj_up_in.T,
        proj_up_out.T,
        store,
        layer_mask.T,
    )
    scores = scores.reshape(n_grp, q_pad, out_width)[:, :nq].reshape(n_grp * nq, out_width)
    slot = lax.axis_index("col") * out_width + jnp.arange(out_width, dtype=jnp.int32)
    return jnp.where((slot < live_count[0])[None, :], scores, 0.0)


def solution(mesh):
    return jax.shard_map(
        local,
        mesh=mesh,
        in_specs=(
            P("grp", "col"),
            P("grp", "col"),
            P("col", "doc"),
            P("col", "doc"),
            P("doc", "col"),
            P("doc", None),
            P("col", None),
            P("col", None),
            P("doc", None),
            P(("grp", "doc"), "col"),
            P(("grp", "doc"), None),
            P(("grp", "doc")),
        ),
        out_specs=P(None, ("grp", "doc", "col")),
        check_vma=False,
    )
```

```python
import functools
import math

import jax
import jax.numpy as jnp
from jax import lax
from jax.experimental import pallas as pl
from jax.experimental.pallas import tpu as pltpu
from jax.sharding import PartitionSpec as P

MESH = pl.DeviceIdType.MESH
SEQ = 256
LANES = 128
EPSILON = 1e-06
NT = (((1,), (1,)), ((), ()))
f32, bf16 = jnp.float32, jnp.bfloat16


def dot(left, right):
    return jnp.dot(left, right, preferred_element_type=f32)


def dot_nt(left, right):
    return lax.dot_general(left, right, NT, preferred_element_type=f32)


def kernel(
    sizes,
    x_in,
    og_in,
    wg_in,
    wu_in,
    wd_in,
    pdi_in,
    pdo_in,
    pui_in,
    puo_in,
    store_in,
    mask_in,
    out_ref,
    x,
    og,
    wg,
    wu,
    wd,
    pdi,
    pdo,
    pui,
    puo,
    store,
    mask,
    gate,
    up,
    hg,
    s,
    send_a,
    recv_a,
    send_b,
    recv_b,
    ends_part,
    ends_recv,
    ends,
    ends_t,
    ui2,
    pairs,
    grads,
    grads_send,
    x_recv,
    block,
    block_send,
    d_recv,
    full,
    select,
    norm_send,
    norm_recv,
    c_send,
    c_recv,
    load_sem,
    x_load_sem,
    ring_s,
    ring_r,
    ends_s,
    ends_r,
    gather_s,
    gather_r,
    x_s,
    x_r,
    d_s,
    d_r,
    g_s,
    g_r,
    norm_s,
    norm_r,
    c_s,
    c_r,
):
    n_grp, n_doc, n_col, nq = sizes
    part = SEQ // n_col
    half = part // 2
    early = nq // 2
    batches = ((0, early), (early, nq - 1 - early), (nq - 1, 1))
    g, d, c = lax.axis_index("grp"), lax.axis_index("doc"), lax.axis_index("col")
    right, left, across = (
        lax.rem(c + 1, n_col),
        lax.rem(c + n_col - 1, n_col),
        lax.rem(c + 2, n_col),
    )
    k_dim = pdi_in.shape[0]

    def remote(src, dst, send, recv, **place):
        return pltpu.make_async_remote_copy(
            src_ref=src,
            dst_ref=dst,
            send_sem=send,
            recv_sem=recv,
            device_id=place,
            device_id_type=MESH,
        )

    def token_rows(p):
        return pl.ds(pl.multiple_of(p * SEQ, SEQ), SEQ)

    def own_rows(owner, first, count):
        return pl.ds(pl.multiple_of(owner * part + first, half), count)

    loads = {}

    def load(key, src, dst):
        copy = pltpu.make_async_copy(src, dst, load_sem.at[len(loads)])
        copy.start()
        loads[key] = copy

    def x_load(p):
        return pltpu.make_async_copy(
            x_in.at[token_rows(p)], x.at[token_rows(p)], x_load_sem.at[p]
        )

    load("wg", wg_in, wg)
    for p in range(nq):
        x_load(p).start()

    barrier = pltpu.get_barrier_semaphore()
    for k in range(1, n_col):
        pl.semaphore_signal(
            barrier, 1, device_id={"col": lax.rem(c + k, n_col)}, device_id_type=MESH
        )
    for k in range(1, n_grp):
        pl.semaphore_signal(
            barrier, 1, device_id={"grp": lax.rem(g + k, n_grp)}, device_id_type=MESH
        )

    def greet(k, carry):
        pl.semaphore_signal(
            barrier, 1, device_id={"doc": lax.rem(d + k, n_doc)}, device_id_type=MESH
        )
        return carry

    lax.fori_loop(1, n_doc, greet, 0)

    loads["wg"].wait()
    x_load(0).wait()
    load("og", og_in, og)
    load("pdo", pdo_in, pdo.at[pl.ds(0, k_dim)])
    load("pui", pui_in, pui.at[pl.ds(k_dim, k_dim)])
    load("wu", wu_in, wu)
    load("wd", wd_in, wd)
    load("store", store_in, store)
    load("mask", mask_in, mask)
    load("pdi", pdi_in, pdi.at[pl.ds(0, k_dim)])
    load("pdi2", pdi_in, pdi.at[pl.ds(k_dim, k_dim)])
    load("puo", puo_in, puo)

    def gate_term(p):
        gate[p] = dot(x[token_rows(p)], wg[...])
        send_a[p] = gate[p, own_rows(across, 0, part)].astype(bf16)

    gate_term(0)
    pl.semaphore_wait(barrier, n_col + n_grp + n_doc - 3)

    def copy_a(p, way):
        rows = pl.ds(way * half, half)
        return remote(
            send_a.at[p, rows],
            recv_a.at[p, way],
            ring_s.at[0, p, way],
            ring_r.at[0, p, way],
            col=(right, left)[way],
        )

    def copy_b(p, way):
        return remote(
            send_b.at[p, way],
            recv_b.at[p, way],
            ring_s.at[1, p, way],
            ring_r.at[1, p, way],
            col=(right, left)[way],
        )

    def copy_g(p, way, slot):
        return remote(
            s.at[p, slot],
            s.at[p, slot],
            ring_s.at[2, p, way],
            ring_r.at[2, p, way],
            col=(right, left)[way],
        )

    def copy_f(p, way, slot):
        rows = pl.ds(way * half, half)
        return remote(
            s.at[p, slot, rows],
            s.at[p, slot, rows],
            ring_s.at[3, p, way],
            ring_r.at[3, p, way],
            col=(right, left)[way],
        )

    copy_a(0, 0).start()
    copy_a(0, 1).start()

    def gate_step(p, carry):
        x_load(p).wait()
        gate_term(p)
        copy_a(p, 0).start()
        copy_a(p, 1).start()
        return carry

    lax.fori_loop(1, nq, gate_step, 0)

    slab = ends_part.shape[0]
    loads["og"].wait()
    loads["pdo"].wait()
    loads["pui"].wait()
    pdo[pl.ds(k_dim, k_dim)] = jnp.zeros((k_dim, pdo.shape[1]), bf16)
    pui[pl.ds(0, k_dim)] = jnp.zeros((k_dim, pui.shape[1]), bf16)
    mine = pl.ds(pl.multiple_of(d * slab, slab), slab)
    ends_part[...] = (dot_nt(og[mine], pdo[...]) + dot_nt(x[mine], pui[...])).astype(bf16)

    def copy_ends(k):
        return remote(
            ends_part,
            ends_recv.at[k - 1],
            ends_s.at[k - 1],
            ends_r.at[k - 1],
            col=lax.rem(c + k, n_col),
        )

    for k in range(1, n_col):
        copy_ends(k).start()

    loads["wu"].wait()
    loads["wd"].wait()

    def terms_step(p, carry):
        up[p] = dot(x[token_rows(p)], wu[...]).astype(bf16)
        copy_a(p, 0).wait_recv()
        send_b[p, 0, pl.ds(0, half)] = (
            gate[p, own_rows(right, 0, half)] + recv_a[p, 0].astype(f32)
        ).astype(bf16)
        send_b[p, 0, pl.ds(half, half)] = gate[p, own_rows(right, half, half)].astype(bf16)
        copy_b(p, 0).start()
        copy_a(p, 1).wait_recv()
        send_b[p, 1, pl.ds(0, half)] = gate[p, own_rows(left, 0, half)].astype(bf16)
        send_b[p, 1, pl.ds(half, half)] = (
            gate[p, own_rows(left, half, half)] + recv_a[p, 1].astype(f32)
        ).astype(bf16)
        copy_b(p, 1).start()
        hg[p] = dot_nt(og[token_rows(p)], wd[...]).astype(bf16)
        return carry

    lax.fori_loop(0, nq, terms_step, 0)

    for k in range(1, n_col):
        copy_ends(k).wait_recv()
    total = ends_part[...].astype(f32)
    for k in range(1, n_col):
        total += ends_recv[k - 1].astype(f32)
    ends[mine] = total.astype(bf16)

    def copy_gather(k, owner):
        rows = pl.ds(pl.multiple_of(owner * slab, slab), slab)
        return remote(
            ends.at[rows],
            ends.at[rows],
            gather_s.at[k - 1],
            gather_r.at[k - 1],
            doc=lax.rem(d + k, n_doc),
        )

    def gather_start(k, carry):
        copy_gather(k, d).start()
        return carry

    lax.fori_loop(1, n_doc, gather_start, 0)

    loads["store"].wait()
    squares = jnp.zeros((store.shape[0], LANES), f32)
    for j in range(store.shape[1] // LANES):
        value = store[:, pl.ds(j * LANES, LANES)].astype(f32)
        squares += value * value
    upper = squares.astype(bf16)
    lower = (squares - upper.astype(f32)).astype(bf16)
    ones = jnp.ones((8, LANES), bf16)
    doc_squares = dot_nt(ones, upper) + dot_nt(ones, lower)
    loads["mask"].wait()
    keep = jnp.where(c < n_col // 2, mask[0:1, :], mask[1:2, :]).astype(f32)
    doc_squares = doc_squares * keep
    out_width = store.shape[0] // n_col
    for j in range(n_col):
        norm_send[j] = doc_squares[:, j * out_width : (j + 1) * out_width]

    def copy_norm(k):
        to = lax.rem(c + k, n_col)
        return remote(
            norm_send.at[to], norm_recv.at[k - 1], norm_s.at[k - 1], norm_r.at[k - 1], col=to
        )

    def own_step(p, carry):
        copy_b(p, 0).wait_recv()
        copy_b(p, 1).wait_recv()
        value = (
            gate[p, own_rows(c, 0, part)] + recv_b[p, 0].astype(f32) + recv_b[p, 1].astype(f32)
        )
        s[p, c] = (value * jax.nn.sigmoid(value)).astype(bf16)
        copy_g(p, 0, c).start()
        copy_g(p, 1, c).start()
        return carry

    lax.fori_loop(0, early, own_step, 0)
    for k in range(1, n_col):
        copy_norm(k).start()

    n_query = n_grp * nq
    n_sub = full.shape[2]
    row = lax.broadcasted_iota(jnp.int32, select.shape, 0)
    lane = lax.broadcasted_iota(jnp.int32, select.shape, 1)
    select[...] = jnp.where(
        row == (lane % n_sub) * n_query + lane // n_sub, 1.0, 0.0
    ).astype(bf16)

    def gather_wait(k, carry):
        copy_gather(k, lax.rem(d + n_doc - k, n_doc)).wait_recv()
        return carry

    lax.fori_loop(1, n_doc, gather_wait, 0)
    low_lanes = lax.broadcasted_iota(jnp.int32, (SEQ, LANES), 1) < k_dim

    def ends_step(p, carry):
        value = ends[token_rows(p)].astype(f32)
        ends_t[p] = value.T[:k_dim].astype(bf16)
        ui2[p] = jnp.where(low_lanes, pltpu.roll(value, k_dim, 1), value).astype(bf16)
        return carry

    lax.fori_loop(0, nq, ends_step, 0)

    def forward_step(p, carry):
        copy_g(p, 0, left).wait_recv()
        copy_f(p, 0, left).start()
        copy_g(p, 1, right).wait_recv()
        copy_f(p, 1, right).start()
        return carry

    lax.fori_loop(0, early - 1, forward_step, 0)
    lax.fori_loop(early, early + 1, own_step, 0)
    lax.fori_loop(early - 1, early, forward_step, 0)
    lax.fori_loop(early + 1, nq, own_step, 0)

    loads["pdi"].wait()
    loads["pdi2"].wait()
    loads["puo"].wait()
    low_half = lax.broadcasted_iota(jnp.int32, (k_dim // 2, LANES), 1) < k_dim

    def grads_step(p, carry):
        copy_f(p, 0, across).wait_recv()
        copy_f(p, 1, across).wait_recv()
        shared = s[p].reshape(SEQ, s.shape[-1])
        down_in = dot_nt(up[p] * shared, pdi[...])
        up_out = dot_nt(puo[...], hg[p] * shared)
        pairs[pl.ds(0, k_dim)] = dot(ends_t[p], down_in.astype(bf16))
        pairs[pl.ds(k_dim, k_dim)] = dot(up_out.astype(bf16), ui2[p])
        for m in range(2):
            even = pairs[pl.ds(m * k_dim, k_dim // 2, 2)]
            odd = pairs[pl.ds(m * k_dim + 1, k_dim // 2, 2)]
            value = jnp.where(low_half, even, odd)
            grads[p, pl.ds(m * (k_dim // 2), k_dim // 2)] = value
            grads_send[p, pl.ds(m * (k_dim // 2), k_dim // 2)] = value.astype(bf16)
        return carry

    def copy_x(batch, k):
        first, count = batches[batch]
        to = lax.rem(c + k, n_col)
        return remote(
            grads_send.at[
                pl.ds(first, count), pl.ds(pl.multiple_of(to * n_sub, n_sub), n_sub)
            ],
            x_recv.at[k - 1, pl.ds(first, count)],
            x_s.at[batch, k - 1],
            x_r.at[batch, k - 1],
            col=to,
        )

    def copy_d(batch, k):
        first, count = batches[batch]
        return remote(
            block_send.at[pl.ds(first, count)],
            d_recv.at[k - 1, pl.ds(first, count)],
            d_s.at[batch, k - 1],
            d_r.at[batch, k - 1],
            doc=lax.rem(d + k, n_doc),
        )

    def copy_grp(batch, k, owner):
        first, count = batches[batch]
        return remote(
            full.at[owner, pl.ds(first, count)],
            full.at[owner, pl.ds(first, count)],
            g_s.at[batch, k - 1],
            g_r.at[batch, k - 1],
            grp=lax.rem(g + k, n_grp),
        )

    def make_grads(batch):
        first, count = batches[batch]
        lax.fori_loop(first, first + count, grads_step, 0)
        for k in range(1, n_col):
            copy_x(batch, k).start()

    def sum_col(batch):
        first, count = batches[batch]
        span = pl.ds(first, count)
        for k in range(1, n_col):
            copy_x(batch, k).wait_recv()
        total = grads[span, pl.ds(pl.multiple_of(c * n_sub, n_sub), n_sub)]
        for k in range(1, n_col):
            total += x_recv[k - 1, span].astype(f32)
        block[span] = total
        block_send[span] = total.astype(bf16)

        def start(k, carry):
            copy_d(batch, k).start()
            return carry

        lax.fori_loop(1, n_doc, start, 0)

    def sum_doc(batch):
        first, count = batches[batch]
        span = pl.ds(first, count)

        def wait(k, carry):
            copy_d(batch, k).wait_recv()
            return carry

        lax.fori_loop(1, n_doc, wait, 0)
        total = block[span]
        for k in range(1, n_doc):
            total += d_recv[k - 1, span].astype(f32)
        full[g, span] = total.astype(bf16)
        for k in range(1, n_grp):
            copy_grp(batch, k, g).start()

    make_grads(0)
    lax.fori_loop(early, nq, forward_step, 0)
    sum_col(0)
    make_grads(1)
    make_grads(2)
    sum_col(1)
    sum_col(2)
    sum_doc(0)
    sum_doc(1)
    sum_doc(2)
    for batch in range(len(batches)):
        for k in range(1, n_grp):
            copy_grp(batch, k, lax.rem(g + n_grp - k, n_grp)).wait_recv()

    ordered = dot(select[...], full[...].reshape(n_query * n_sub, LANES))
    query = jnp.concatenate(
        [ordered[kk * n_query : (kk + 1) * n_query] for kk in range(n_sub)], axis=1
    )
    raw = dot_nt(query.astype(bf16), store[...]) * keep
    query_squares = jnp.broadcast_to(
        jnp.sum(query * query, axis=1, keepdims=True), (n_query, out_width)
    )
    for j in range(n_col):
        c_send[j, pl.ds(0, n_query)] = raw[:, j * out_width : (j + 1) * out_width]
        c_send[j, pl.ds(n_query, n_query)] = query_squares

    def copy_c(k):
        to = lax.rem(c + k, n_col)
        return remote(c_send.at[to], c_recv.at[k - 1], c_s.at[k - 1], c_r.at[k - 1], col=to)

    for k in range(1, n_col):
        copy_c(k).start()
    norms = norm_send[c]
    for k in range(1, n_col):
        copy_norm(k).wait_recv()
        norms += norm_recv[k - 1]
    columns = float(n_col * n_sub * LANES)
    doc_norm = jnp.sqrt(norms[0:1] / columns + EPSILON) * math.sqrt(columns)
    total = c_send[c]
    for k in range(1, n_col):
        copy_c(k).wait_recv()
    for k in range(1, n_col):
        total += c_recv[k - 1]
    query_norm = jnp.sqrt(total[n_query:] / columns + EPSILON)
    out_ref[...] = total[:n_query] / (query_norm * doc_norm)

    def ring_done(p, carry):
        for way in range(2):
            copy_a(p, way).wait_send()
            copy_b(p, way).wait_send()
            copy_g(p, way, c).wait_send()
            copy_f(p, way, left).wait_send()
        return carry

    lax.fori_loop(0, nq, ring_done, 0)

    def doc_done(k, carry):
        copy_gather(k, d).wait_send()
        for batch in range(len(batches)):
            copy_d(batch, k).wait_send()
        return carry

    lax.fori_loop(1, n_doc, doc_done, 0)
    for k in range(1, n_col):
        copy_ends(k).wait_send()
        copy_norm(k).wait_send()
        copy_c(k).wait_send()
        for batch in range(len(batches)):
            copy_x(batch, k).wait_send()
    for k in range(1, n_grp):
        for batch in range(len(batches)):
            copy_grp(batch, k, g).wait_send()


def local(
    mlp_input,
    out_grad,
    w_gate,
    w_up,
    w_down,
    proj_down_in,
    proj_down_out,
    proj_up_in,
    proj_up_out,
    store,
    layer_mask,
    live_count,
):
    n_grp, n_doc, n_col = (lax.axis_size(name) for name in ("grp", "doc", "col"))
    tokens, depth = mlp_input.shape
    width = w_gate.shape[1]
    k_dim = proj_down_in.shape[1]
    nq = tokens // SEQ
    part = SEQ // n_col
    slab = tokens // n_doc
    n_row = 2 * k_dim * k_dim // LANES
    n_sub = n_row // n_col
    out_width = store.shape[0] // n_col
    dma = pltpu.SemaphoreType.DMA
    scratch = [
        pltpu.VMEM((tokens, depth), bf16),
        pltpu.VMEM((tokens, depth), bf16),
        pltpu.VMEM((depth, width), bf16),
        pltpu.VMEM((depth, width), bf16),
        pltpu.VMEM((width, depth), bf16),
        pltpu.VMEM((2 * k_dim, width), bf16),
        pltpu.VMEM((2 * k_dim, depth), bf16),
        pltpu.VMEM((2 * k_dim, depth), bf16),
        pltpu.VMEM((k_dim, width), bf16),
        pltpu.VMEM(store.shape, bf16),
        pltpu.VMEM(layer_mask.shape[::-1], jnp.int32),
        pltpu.VMEM((nq, SEQ, width), f32),
        pltpu.VMEM((nq, SEQ, width), bf16),
        pltpu.VMEM((nq, SEQ, width), bf16),
        pltpu.VMEM((nq, n_col, part, width), bf16),
        pltpu.VMEM((nq, part, width), bf16),
        pltpu.VMEM((nq, 2, part // 2, width), bf16),
        pltpu.VMEM((nq, 2, part, width), bf16),
        pltpu.VMEM((nq, 2, part, width), bf16),
        pltpu.VMEM((slab, LANES), bf16),
        pltpu.VMEM((n_col - 1, slab, LANES), bf16),
        pltpu.VMEM((tokens, LANES), bf16),
        pltpu.VMEM((nq, k_dim, SEQ), bf16),
        pltpu.VMEM((nq, SEQ, LANES), bf16),
        pltpu.VMEM((2 * k_dim, LANES), f32),
        pltpu.VMEM((nq, n_row, LANES), f32),
        pltpu.VMEM((nq, n_row, LANES), bf16),
        pltpu.VMEM((n_col - 1, nq, n_sub, LANES), bf16),
        pltpu.VMEM((nq, n_sub, LANES), f32),
        pltpu.VMEM((nq, n_sub, LANES), bf16),
        pltpu.VMEM((n_doc - 1, nq, n_sub, LANES), bf16),
        pltpu.VMEM((n_grp, nq, n_sub, LANES), bf16),
        pltpu.VMEM((n_grp * nq * n_sub, n_grp * nq * n_sub), bf16),
        pltpu.VMEM((n_col, 8, out_width), f32),
        pltpu.VMEM((n_col - 1, 8, out_width), f32),
        pltpu.VMEM((n_col, 2 * n_grp * nq, out_width), f32),
        pltpu.VMEM((n_col - 1, 2 * n_grp * nq, out_width), f32),
        dma((11,)),
        dma((nq,)),
        dma((4, nq, 2)),
        dma((4, nq, 2)),
        dma((n_col - 1,)),
        dma((n_col - 1,)),
        dma((n_doc - 1,)),
        dma((n_doc - 1,)),
        dma((3, n_col - 1)),
        dma((3, n_col - 1)),
        dma((3, n_doc - 1)),
        dma((3, n_doc - 1)),
        dma((3, n_grp - 1)),
        dma((3, n_grp - 1)),
        dma((n_col - 1,)),
        dma((n_col - 1,)),
        dma((n_col - 1,)),
        dma((n_col - 1,)),
    ]
    scores = pl.pallas_call(
        functools.partial(kernel, (n_grp, n_doc, n_col, nq)),
        out_shape=jax.ShapeDtypeStruct((n_grp * nq, out_width), f32),
        in_specs=[pl.BlockSpec(memory_space=pl.ANY)] * 11,
        out_specs=pl.BlockSpec(memory_space=pltpu.VMEM),
        scratch_shapes=scratch,
        compiler_params=pltpu.CompilerParams(
            collective_id=0, has_side_effects=True, vmem_limit_bytes=58 * 1024 * 1024
        ),
        cost_estimate=pl.CostEstimate(
            flops=6 * tokens * depth * width, bytes_accessed=14 << 20, transcendentals=0
        ),
    )(
        mlp_input,
        out_grad,
        w_gate,
        w_up,
        w_down,
        proj_down_in.T,
        proj_down_out.T,
        proj_up_in.T,
        proj_up_out.T,
        store,
        layer_mask.T,
    )
    slot = lax.axis_index("col") * out_width + jnp.arange(out_width, dtype=jnp.int32)
    return jnp.where((slot < live_count[0])[None, :], scores, 0.0)


def solution(mesh):
    return jax.shard_map(
        local,
        mesh=mesh,
        in_specs=(
            P("grp", "col"),
            P("grp", "col"),
            P("col", "doc"),
            P("col", "doc"),
            P("doc", "col"),
            P("doc", None),
            P("col", None),
            P("col", None),
            P("doc", None),
            P(("grp", "doc"), "col"),
            P(("grp", "doc"), None),
            P(("grp", "doc")),
        ),
        out_specs=P(None, ("grp", "doc", "col")),
        check_vma=False,
    )
```

```python
import functools
import math

import jax
import jax.numpy as jnp
from jax import lax
from jax.experimental import pallas as pl
from jax.experimental.pallas import tpu as pltpu
from jax.sharding import PartitionSpec as P

MESH = pl.DeviceIdType.MESH
SEQ = 256
LANES = 128
EPSILON = 1e-06
NT = (((1,), (1,)), ((), ()))
f32, bf16 = jnp.float32, jnp.bfloat16


def dot(left, right):
    return jnp.dot(left, right, preferred_element_type=f32)


def dot_nt(left, right):
    return lax.dot_general(left, right, NT, preferred_element_type=f32)


def kernel(
    sizes,
    x_in,
    og_in,
    wg_in,
    wu_in,
    wd_in,
    pdi_in,
    pdo_in,
    pui_in,
    puo_in,
    store_in,
    mask_in,
    live_in,
    out_ref,
    x,
    og,
    wg,
    wu,
    wd,
    pdi,
    pdo,
    pui,
    puo,
    store,
    mask,
    live,
    gate,
    up,
    hg,
    s,
    send_a,
    recv_a,
    send_b,
    recv_b,
    ends_part,
    ends_recv,
    ends,
    ends_t,
    ui2,
    pairs,
    grads,
    grads_send,
    x_recv,
    block,
    block_send,
    z_recv,
    y_send,
    y_recv,
    full,
    select,
    norm_send,
    norm_recv,
    c_send,
    c_recv,
    load_sem,
    x_load_sem,
    ring_s,
    ring_r,
    ends_s,
    ends_r,
    gather_s,
    gather_r,
    pair_s,
    pair_r,
    x_s,
    x_r,
    z_s,
    z_r,
    y_s,
    y_r,
    norm_s,
    norm_r,
    c_s,
    c_r,
):
    n_grp, n_doc, n_col, nq = sizes
    part = SEQ // n_col
    half = part // 2
    early = nq // 2
    batches = ((0, early), (early, nq - 1 - early), (nq - 1, 1))
    g, d, c = lax.axis_index("grp"), lax.axis_index("doc"), lax.axis_index("col")
    right, left, across = (
        lax.rem(c + 1, n_col),
        lax.rem(c + n_col - 1, n_col),
        lax.rem(c + 2, n_col),
    )
    n_z = n_doc // 2
    z, upper_y = d // 2, lax.rem(d, 2)
    k_dim = pdi_in.shape[0]

    def along_z(k):
        return {"doc": lax.rem(z + k, n_z) * 2 + upper_y}

    def along_y(j, e):
        return {"grp": lax.rem(g + j, n_grp), "doc": z * 2 + (upper_y + e - 2 * upper_y * e)}

    y_steps = [(j, e) for j in range(n_grp) for e in range(2) if j or e]

    def remote(src, dst, send, recv, **place):
        return pltpu.make_async_remote_copy(
            src_ref=src,
            dst_ref=dst,
            send_sem=send,
            recv_sem=recv,
            device_id=place,
            device_id_type=MESH,
        )

    def token_rows(p):
        return pl.ds(pl.multiple_of(p * SEQ, SEQ), SEQ)

    def own_rows(owner, first, count):
        return pl.ds(pl.multiple_of(owner * part + first, half), count)

    loads = {}

    def load(key, src, dst):
        copy = pltpu.make_async_copy(src, dst, load_sem.at[len(loads)])
        copy.start()
        loads[key] = copy

    def x_load(p):
        return pltpu.make_async_copy(
            x_in.at[token_rows(p)], x.at[token_rows(p)], x_load_sem.at[p]
        )

    load("wg", wg_in, wg)
    x_load(0).start()

    barrier = pltpu.get_barrier_semaphore()

    def greet(place):
        pl.semaphore_signal(barrier, 1, device_id=place, device_id_type=MESH)

    for k in sorted(range(1, n_z), key=lambda k: -min(k, n_z - k)):
        greet(along_z(k))
    for j, e in sorted(y_steps, key=lambda step: -step[1]):
        greet(along_y(j, e))
    for k in range(1, n_col):
        greet({"col": lax.rem(c + k, n_col)})
    for p in range(1, nq):
        x_load(p).start()

    loads["wg"].wait()
    x_load(0).wait()
    load("og", og_in, og)
    load("pdo", pdo_in, pdo.at[pl.ds(0, k_dim)])
    load("pui", pui_in, pui.at[pl.ds(k_dim, k_dim)])
    load("wu", wu_in, wu)
    load("wd", wd_in, wd)
    load("store", store_in, store)
    load("mask", mask_in, mask)
    load("pdi", pdi_in, pdi.at[pl.ds(0, k_dim)])
    load("pdi2", pdi_in, pdi.at[pl.ds(k_dim, k_dim)])
    load("puo", puo_in, puo)
    load("live", live_in, live)

    def gate_term(p):
        gate[p] = dot(x[token_rows(p)], wg[...])
        send_a[p] = gate[p, own_rows(across, 0, part)].astype(bf16)

    gate_term(0)
    pl.semaphore_wait(barrier, n_z - 1 + len(y_steps) + n_col - 1)

    def copy_a(p, way):
        rows = pl.ds(way * half, half)
        return remote(
            send_a.at[p, rows],
            recv_a.at[p, way],
            ring_s.at[0, p, way],
            ring_r.at[0, p, way],
            col=(right, left)[way],
        )

    def copy_b(p, way):
        return remote(
            send_b.at[p, way],
            recv_b.at[p, way],
            ring_s.at[1, p, way],
            ring_r.at[1, p, way],
            col=(right, left)[way],
        )

    def copy_g(p, way, slot):
        return remote(
            s.at[p, slot],
            s.at[p, slot],
            ring_s.at[2, p, way],
            ring_r.at[2, p, way],
            col=(right, left)[way],
        )

    def copy_f(p, way, slot):
        rows = pl.ds(way * half, half)
        return remote(
            s.at[p, slot, rows],
            s.at[p, slot, rows],
            ring_s.at[3, p, way],
            ring_r.at[3, p, way],
            col=(right, left)[way],
        )

    copy_a(0, 0).start()
    copy_a(0, 1).start()

    def gate_step(p, carry):
        x_load(p).wait()
        gate_term(p)
        copy_a(p, 0).start()
        copy_a(p, 1).start()
        return carry

    lax.fori_loop(1, nq, gate_step, 0)

    slab = ends_part.shape[0]
    loads["og"].wait()
    loads["pdo"].wait()
    loads["pui"].wait()
    pdo[pl.ds(k_dim, k_dim)] = jnp.zeros((k_dim, pdo.shape[1]), bf16)
    pui[pl.ds(0, k_dim)] = jnp.zeros((k_dim, pui.shape[1]), bf16)
    mine = pl.ds(pl.multiple_of((upper_y * n_z + z) * slab, slab), slab)
    ends_part[...] = (dot_nt(og[mine], pdo[...]) + dot_nt(x[mine], pui[...])).astype(bf16)

    def copy_ends(k):
        return remote(
            ends_part,
            ends_recv.at[k - 1],
            ends_s.at[k - 1],
            ends_r.at[k - 1],
            col=lax.rem(c + k, n_col),
        )

    for k in range(1, n_col):
        copy_ends(k).start()

    loads["wu"].wait()
    loads["wd"].wait()

    def terms_step(p, carry):
        up[p] = dot(x[token_rows(p)], wu[...]).astype(bf16)
        copy_a(p, 0).wait_recv()
        send_b[p, 0, pl.ds(0, half)] = (
            gate[p, own_rows(right, 0, half)] + recv_a[p, 0].astype(f32)
        ).astype(bf16)
        send_b[p, 0, pl.ds(half, half)] = gate[p, own_rows(right, half, half)].astype(bf16)
        copy_b(p, 0).start()
        copy_a(p, 1).wait_recv()
        send_b[p, 1, pl.ds(0, half)] = gate[p, own_rows(left, 0, half)].astype(bf16)
        send_b[p, 1, pl.ds(half, half)] = (
            gate[p, own_rows(left, half, half)] + recv_a[p, 1].astype(f32)
        ).astype(bf16)
        copy_b(p, 1).start()
        hg[p] = dot_nt(og[token_rows(p)], wd[...]).astype(bf16)
        return carry

    lax.fori_loop(0, nq, terms_step, 0)

    for k in range(1, n_col):
        copy_ends(k).wait_recv()
    total = ends_part[...].astype(f32)
    for k in range(1, n_col):
        total += ends_recv[k - 1].astype(f32)
    ends[mine] = total.astype(bf16)

    def copy_gather(k, owner):
        rows = pl.ds(pl.multiple_of((upper_y * n_z + owner) * slab, slab), slab)
        return remote(
            ends.at[rows],
            ends.at[rows],
            gather_s.at[k - 1],
            gather_r.at[k - 1],
            **along_z(k),
        )

    def copy_pair(owner):
        rows = pl.ds(pl.multiple_of(owner * n_z * slab, n_z * slab), n_z * slab)
        return remote(ends.at[rows], ends.at[rows], pair_s, pair_r, **along_y(0, 1))

    for k in range(1, n_z):
        copy_gather(k, z).start()

    loads["store"].wait()
    squares = jnp.zeros((store.shape[0], LANES), f32)
    for j in range(store.shape[1] // LANES):
        value = store[:, pl.ds(j * LANES, LANES)].astype(f32)
        squares += value * value
    upper = squares.astype(bf16)
    lower = (squares - upper.astype(f32)).astype(bf16)
    ones = jnp.ones((8, LANES), bf16)
    doc_squares = dot_nt(ones, upper) + dot_nt(ones, lower)
    loads["mask"].wait()
    keep = jnp.where(c < n_col // 2, mask[0:1, :], mask[1:2, :]).astype(f32)
    doc_squares = doc_squares * keep
    out_width = store.shape[0] // n_col
    for j in range(n_col):
        norm_send[j] = doc_squares[:, j * out_width : (j + 1) * out_width]

    def copy_norm(k):
        to = lax.rem(c + k, n_col)
        return remote(
            norm_send.at[to], norm_recv.at[k - 1], norm_s.at[k - 1], norm_r.at[k - 1], col=to
        )

    def own_step(p, carry):
        copy_b(p, 0).wait_recv()
        copy_b(p, 1).wait_recv()
        value = (
            gate[p, own_rows(c, 0, part)] + recv_b[p, 0].astype(f32) + recv_b[p, 1].astype(f32)
        )
        s[p, c] = (value * jax.nn.sigmoid(value)).astype(bf16)
        copy_g(p, 0, c).start()
        copy_g(p, 1, c).start()
        return carry

    def forward_step(p, carry):
        copy_g(p, 0, left).wait_recv()
        copy_f(p, 0, left).start()
        copy_g(p, 1, right).wait_recv()
        copy_f(p, 1, right).start()
        return carry

    lax.fori_loop(0, early, own_step, 0)
    for k in range(1, n_col):
        copy_norm(k).start()

    n_query = n_grp * nq
    n_sub = full.shape[2]
    row = lax.broadcasted_iota(jnp.int32, select.shape, 0)
    lane = lax.broadcasted_iota(jnp.int32, select.shape, 1)
    select[...] = jnp.where(
        row == (lane % n_sub) * n_query + lane // n_sub, 1.0, 0.0
    ).astype(bf16)

    for k in range(1, n_z):
        copy_gather(k, lax.rem(z + n_z - k, n_z)).wait_recv()
    copy_pair(upper_y).start()
    lax.fori_loop(0, early - 1, forward_step, 0)
    copy_pair(1 - upper_y).wait_recv()
    low_lanes = lax.broadcasted_iota(jnp.int32, (SEQ, LANES), 1) < k_dim

    def ends_step(p, carry):
        value = ends[token_rows(p)].astype(f32)
        ends_t[p] = value.T[:k_dim].astype(bf16)
        ui2[p] = jnp.where(low_lanes, pltpu.roll(value, k_dim, 1), value).astype(bf16)
        return carry

    lax.fori_loop(0, nq, ends_step, 0)

    lax.fori_loop(early, early + 1, own_step, 0)
    lax.fori_loop(early - 1, early, forward_step, 0)
    lax.fori_loop(early + 1, nq, own_step, 0)

    loads["pdi"].wait()
    loads["pdi2"].wait()
    loads["puo"].wait()
    low_half = lax.broadcasted_iota(jnp.int32, (k_dim // 2, LANES), 1) < k_dim

    def grads_step(p, carry):
        copy_f(p, 0, across).wait_recv()
        copy_f(p, 1, across).wait_recv()
        shared = s[p].reshape(SEQ, s.shape[-1])
        down_in = dot_nt(up[p] * shared, pdi[...])
        up_out = dot_nt(puo[...], hg[p] * shared)
        pairs[pl.ds(0, k_dim)] = dot(ends_t[p], down_in.astype(bf16))
        pairs[pl.ds(k_dim, k_dim)] = dot(up_out.astype(bf16), ui2[p])
        for m in range(2):
            even = pairs[pl.ds(m * k_dim, k_dim // 2, 2)]
            odd = pairs[pl.ds(m * k_dim + 1, k_dim // 2, 2)]
            value = jnp.where(low_half, even, odd)
            grads[p, pl.ds(m * (k_dim // 2), k_dim // 2)] = value
            grads_send[p, pl.ds(m * (k_dim // 2), k_dim // 2)] = value.astype(bf16)
        return carry

    def copy_x(batch, k):
        first, count = batches[batch]
        to = lax.rem(c + k, n_col)
        return remote(
            grads_send.at[
                pl.ds(first, count), pl.ds(pl.multiple_of(to * n_sub, n_sub), n_sub)
            ],
            x_recv.at[k - 1, pl.ds(first, count)],
            x_s.at[batch, k - 1],
            x_r.at[batch, k - 1],
            col=to,
        )

    def copy_z(batch, k):
        first, count = batches[batch]
        return remote(
            block_send.at[pl.ds(first, count)],
            z_recv.at[k - 1, pl.ds(first, count)],
            z_s.at[batch, k - 1],
            z_r.at[batch, k - 1],
            **along_z(k),
        )

    def copy_y(batch, j, e):
        first, count = batches[batch]
        return remote(
            y_send.at[pl.ds(first, count)],
            y_recv.at[j, e, pl.ds(first, count)],
            y_s.at[batch, j, e],
            y_r.at[batch, j, e],
            **along_y(j, e),
        )

    def make_grads(batch):
        first, count = batches[batch]
        lax.fori_loop(first, first + count, grads_step, 0)
        for k in range(1, n_col):
            copy_x(batch, k).start()

    def sum_col(batch):
        first, count = batches[batch]
        span = pl.ds(first, count)
        for k in range(1, n_col):
            copy_x(batch, k).wait_recv()
        total = grads[span, pl.ds(pl.multiple_of(c * n_sub, n_sub), n_sub)]
        for k in range(1, n_col):
            total += x_recv[k - 1, span].astype(f32)
        block[span] = total
        block_send[span] = total.astype(bf16)

        for k in range(1, n_z):
            copy_z(batch, k).start()

    def sum_z(batch):
        first, count = batches[batch]
        span = pl.ds(first, count)

        for k in range(1, n_z):
            copy_z(batch, k).wait_recv()
        total = block[span]
        for k in range(1, n_z):
            total += z_recv[k - 1, span].astype(f32)
        block[span] = total
        y_send[span] = total.astype(bf16)
        for j, e in y_steps:
            copy_y(batch, j, e).start()

    def sum_y(batch):
        first, count = batches[batch]
        span = pl.ds(first, count)
        for j in range(n_grp):
            copy_y(batch, j, 1).wait_recv()
            if j:
                copy_y(batch, j, 0).wait_recv()
                total = y_recv[j, 0, span].astype(f32)
            else:
                total = block[span]
            total += y_recv[j, 1, span].astype(f32)
            full[lax.rem(g + n_grp - j, n_grp), span] = total.astype(bf16)

    make_grads(0)
    lax.fori_loop(early, nq, forward_step, 0)
    sum_col(0)
    make_grads(1)
    make_grads(2)
    sum_col(1)
    sum_col(2)
    sum_z(0)
    sum_z(1)
    sum_y(0)
    sum_z(2)
    sum_y(1)
    sum_y(2)

    ordered = dot(select[...], full[...].reshape(n_query * n_sub, LANES))
    query = jnp.concatenate(
        [ordered[kk * n_query : (kk + 1) * n_query] for kk in range(n_sub)], axis=1
    )
    raw = dot_nt(query.astype(bf16), store[...]) * keep
    query_squares = jnp.broadcast_to(
        jnp.sum(query * query, axis=1, keepdims=True), (n_query, out_width)
    )
    for j in range(n_col):
        c_send[j, pl.ds(0, n_query)] = raw[:, j * out_width : (j + 1) * out_width]
        c_send[j, pl.ds(n_query, n_query)] = query_squares

    def copy_c(k):
        to = lax.rem(c + k, n_col)
        return remote(c_send.at[to], c_recv.at[k - 1], c_s.at[k - 1], c_r.at[k - 1], col=to)

    for k in range(1, n_col):
        copy_c(k).start()
    norms = norm_send[c]
    for k in range(1, n_col):
        copy_norm(k).wait_recv()
        norms += norm_recv[k - 1]
    columns = float(n_col * n_sub * LANES)
    doc_norm = jnp.sqrt(norms[0:1] / columns + EPSILON) * math.sqrt(columns)
    total = c_send[c]
    for k in range(1, n_col):
        copy_c(k).wait_recv()
    for k in range(1, n_col):
        total += c_recv[k - 1]
    query_norm = jnp.sqrt(total[n_query:] / columns + EPSILON)
    scores = total[:n_query] / (query_norm * doc_norm)
    slot = c * out_width + lax.broadcasted_iota(jnp.int32, scores.shape, 1)
    loads["live"].wait()
    out_ref[...] = jnp.where(slot < live[0], scores, 0.0)

    def ring_done(p, carry):
        for way in range(2):
            copy_a(p, way).wait_send()
            copy_b(p, way).wait_send()
            copy_g(p, way, c).wait_send()
            copy_f(p, way, left).wait_send()
        return carry

    lax.fori_loop(0, nq, ring_done, 0)

    for k in range(1, n_z):
        copy_gather(k, z).wait_send()
        for batch in range(len(batches)):
            copy_z(batch, k).wait_send()
    copy_pair(upper_y).wait_send()
    for k in range(1, n_col):
        copy_ends(k).wait_send()
        copy_norm(k).wait_send()
        copy_c(k).wait_send()
        for batch in range(len(batches)):
            copy_x(batch, k).wait_send()
    for j, e in y_steps:
        for batch in range(len(batches)):
            copy_y(batch, j, e).wait_send()


def local(
    mlp_input,
    out_grad,
    w_gate,
    w_up,
    w_down,
    proj_down_in,
    proj_down_out,
    proj_up_in,
    proj_up_out,
    store,
    layer_mask,
    live_count,
):
    n_grp, n_doc, n_col = (lax.axis_size(name) for name in ("grp", "doc", "col"))
    tokens, depth = mlp_input.shape
    width = w_gate.shape[1]
    k_dim = proj_down_in.shape[1]
    nq = tokens // SEQ
    part = SEQ // n_col
    slab = tokens // n_doc
    n_row = 2 * k_dim * k_dim // LANES
    n_sub = n_row // n_col
    out_width = store.shape[0] // n_col
    dma = pltpu.SemaphoreType.DMA
    scratch = [
        pltpu.VMEM((tokens, depth), bf16),
        pltpu.VMEM((tokens, depth), bf16),
        pltpu.VMEM((depth, width), bf16),
        pltpu.VMEM((depth, width), bf16),
        pltpu.VMEM((width, depth), bf16),
        pltpu.VMEM((2 * k_dim, width), bf16),
        pltpu.VMEM((2 * k_dim, depth), bf16),
        pltpu.VMEM((2 * k_dim, depth), bf16),
        pltpu.VMEM((k_dim, width), bf16),
        pltpu.VMEM(store.shape, bf16),
        pltpu.VMEM(layer_mask.shape[::-1], jnp.int32),
        pltpu.SMEM(live_count.shape, jnp.int32),
        pltpu.VMEM((nq, SEQ, width), f32),
        pltpu.VMEM((nq, SEQ, width), bf16),
        pltpu.VMEM((nq, SEQ, width), bf16),
        pltpu.VMEM((nq, n_col, part, width), bf16),
        pltpu.VMEM((nq, part, width), bf16),
        pltpu.VMEM((nq, 2, part // 2, width), bf16),
        pltpu.VMEM((nq, 2, part, width), bf16),
        pltpu.VMEM((nq, 2, part, width), bf16),
        pltpu.VMEM((slab, LANES), bf16),
        pltpu.VMEM((n_col - 1, slab, LANES), bf16),
        pltpu.VMEM((tokens, LANES), bf16),
        pltpu.VMEM((nq, k_dim, SEQ), bf16),
        pltpu.VMEM((nq, SEQ, LANES), bf16),
        pltpu.VMEM((2 * k_dim, LANES), f32),
        pltpu.VMEM((nq, n_row, LANES), f32),
        pltpu.VMEM((nq, n_row, LANES), bf16),
        pltpu.VMEM((n_col - 1, nq, n_sub, LANES), bf16),
        pltpu.VMEM((nq, n_sub, LANES), f32),
        pltpu.VMEM((nq, n_sub, LANES), bf16),
        pltpu.VMEM((n_doc // 2 - 1, nq, n_sub, LANES), bf16),
        pltpu.VMEM((nq, n_sub, LANES), bf16),
        pltpu.VMEM((n_grp, 2, nq, n_sub, LANES), bf16),
        pltpu.VMEM((n_grp, nq, n_sub, LANES), bf16),
        pltpu.VMEM((n_grp * nq * n_sub, n_grp * nq * n_sub), bf16),
        pltpu.VMEM((n_col, 8, out_width), f32),
        pltpu.VMEM((n_col - 1, 8, out_width), f32),
        pltpu.VMEM((n_col, 2 * n_grp * nq, out_width), f32),
        pltpu.VMEM((n_col - 1, 2 * n_grp * nq, out_width), f32),
        dma((12,)),
        dma((nq,)),
        dma((4, nq, 2)),
        dma((4, nq, 2)),
        dma((n_col - 1,)),
        dma((n_col - 1,)),
        dma((n_doc // 2 - 1,)),
        dma((n_doc // 2 - 1,)),
        dma(()),
        dma(()),
        dma((3, n_col - 1)),
        dma((3, n_col - 1)),
        dma((3, n_doc // 2 - 1)),
        dma((3, n_doc // 2 - 1)),
        dma((3, n_grp, 2)),
        dma((3, n_grp, 2)),
        dma((n_col - 1,)),
        dma((n_col - 1,)),
        dma((n_col - 1,)),
        dma((n_col - 1,)),
    ]
    scores = pl.pallas_call(
        functools.partial(kernel, (n_grp, n_doc, n_col, nq)),
        out_shape=jax.ShapeDtypeStruct((n_grp * nq, out_width), f32),
        in_specs=[pl.BlockSpec(memory_space=pl.ANY)] * 12,
        out_specs=pl.BlockSpec(memory_space=pltpu.VMEM),
        scratch_shapes=scratch,
        compiler_params=pltpu.CompilerParams(
            collective_id=0, has_side_effects=True, vmem_limit_bytes=58 * 1024 * 1024
        ),
        cost_estimate=pl.CostEstimate(
            flops=6 * tokens * depth * width, bytes_accessed=14 << 20, transcendentals=0
        ),
    )(
        mlp_input,
        out_grad,
        w_gate,
        w_up,
        w_down,
        proj_down_in.T,
        proj_down_out.T,
        proj_up_in.T,
        proj_up_out.T,
        store,
        layer_mask.T,
        live_count,
    )
    return scores


def solution(mesh):
    return jax.shard_map(
        local,
        mesh=mesh,
        in_specs=(
            P("grp", "col"),
            P("grp", "col"),
            P("col", "doc"),
            P("col", "doc"),
            P("doc", "col"),
            P("doc", None),
            P("col", None),
            P("col", None),
            P("doc", None),
            P(("grp", "doc"), "col"),
            P(("grp", "doc"), None),
            P(("grp", "doc")),
        ),
        out_specs=P(None, ("grp", "doc", "col")),
        check_vma=False,
    )
```

```python
import functools
import math

import jax
import jax.numpy as jnp
from jax import lax
from jax.experimental import pallas as pl
from jax.experimental.pallas import tpu as pltpu
from jax.sharding import PartitionSpec as P

MESH = pl.DeviceIdType.MESH
SEQ = 256
LANES = 128
EPSILON = 1e-06
NT = (((1,), (1,)), ((), ()))
f32, bf16 = jnp.float32, jnp.bfloat16


def dot(left, right):
    return jnp.dot(left, right, preferred_element_type=f32)


def dot_nt(left, right):
    return lax.dot_general(left, right, NT, preferred_element_type=f32)


def kernel(
    sizes,
    x_in,
    og_in,
    wg_in,
    wu_in,
    wd_in,
    pdi_in,
    pdo_in,
    pui_in,
    puo_in,
    store_in,
    mask_in,
    live_in,
    out_ref,
    x,
    og,
    wg,
    wu,
    wd,
    pdi,
    pdo,
    pui,
    puo,
    store,
    mask,
    live,
    gate,
    up,
    hg,
    s,
    send_a,
    recv_a,
    send_b,
    recv_b,
    ends_part,
    ends_recv,
    ends,
    ends_t,
    ui2,
    pairs,
    grads,
    grads_send,
    x_recv,
    block,
    block_send,
    z_recv,
    y_send,
    y_recv,
    full,
    norm_send,
    norm_recv,
    c_send,
    c_recv,
    load_sem,
    x_load_sem,
    ring_s,
    ring_r,
    ends_s,
    ends_r,
    gather_s,
    gather_r,
    pair_s,
    pair_r,
    x_s,
    x_r,
    z_s,
    z_r,
    y_s,
    y_r,
    norm_s,
    norm_r,
    c_s,
    c_r,
):
    n_grp, n_doc, n_col, nq = sizes
    part = SEQ // n_col
    half = part // 2
    early = nq // 2
    batches = ((0, early), (early, nq - 1 - early), (nq - 1, 1))
    g, d, c = lax.axis_index("grp"), lax.axis_index("doc"), lax.axis_index("col")
    right, left, across = (
        lax.rem(c + 1, n_col),
        lax.rem(c + n_col - 1, n_col),
        lax.rem(c + 2, n_col),
    )
    n_z = n_doc // 2
    z, upper_y = d // 2, lax.rem(d, 2)
    k_dim = pdi_in.shape[0]

    def along_z(k):
        return {"doc": lax.rem(z + k, n_z) * 2 + upper_y}

    def along_y(j, e):
        return {"grp": lax.rem(g + j, n_grp), "doc": z * 2 + (upper_y + e - 2 * upper_y * e)}

    x_steps = sorted(range(1, n_col), key=lambda k: -min(k, n_col - k))
    z_steps = sorted(range(1, n_z), key=lambda k: -min(k, n_z - k))
    y_steps = [(j, e) for e in (1, 0) for j in range(n_grp) if j or e]

    def remote(src, dst, send, recv, **place):
        return pltpu.make_async_remote_copy(
            src_ref=src,
            dst_ref=dst,
            send_sem=send,
            recv_sem=recv,
            device_id=place,
            device_id_type=MESH,
        )

    def token_rows(p):
        return pl.ds(pl.multiple_of(p * SEQ, SEQ), SEQ)

    def own_rows(owner, first, count):
        return pl.ds(pl.multiple_of(owner * part + first, half), count)

    loads = {}

    def load(key, src, dst):
        copy = pltpu.make_async_copy(src, dst, load_sem.at[len(loads)])
        copy.start()
        loads[key] = copy

    def x_load(p):
        return pltpu.make_async_copy(
            x_in.at[token_rows(p)], x.at[token_rows(p)], x_load_sem.at[p]
        )

    load("wg", wg_in, wg)
    x_load(0).start()

    barrier = pltpu.get_barrier_semaphore()

    def greet(place):
        pl.semaphore_signal(barrier, 1, device_id=place, device_id_type=MESH)

    for k in z_steps:
        greet(along_z(k))
    for j, e in y_steps:
        greet(along_y(j, e))
    for k in x_steps:
        greet({"col": lax.rem(c + k, n_col)})
    for p in range(1, nq):
        x_load(p).start()

    loads["wg"].wait()
    x_load(0).wait()
    load("og", og_in, og)
    load("pdo", pdo_in, pdo.at[pl.ds(0, k_dim)])
    load("pui", pui_in, pui.at[pl.ds(k_dim, k_dim)])
    load("wu", wu_in, wu)
    load("wd", wd_in, wd)
    load("store", store_in, store)
    load("mask", mask_in, mask)
    load("pdi", pdi_in, pdi.at[pl.ds(0, k_dim)])
    load("pdi2", pdi_in, pdi.at[pl.ds(k_dim, k_dim)])
    load("puo", puo_in, puo)
    load("live", live_in, live)

    def gate_term(p):
        gate[p] = dot(x[token_rows(p)], wg[...])
        send_a[p] = gate[p, own_rows(across, 0, part)].astype(bf16)

    gate_term(0)
    pl.semaphore_wait(barrier, n_z - 1 + len(y_steps) + n_col - 1)

    def copy_a(p, way):
        rows = pl.ds(way * half, half)
        return remote(
            send_a.at[p, rows],
            recv_a.at[p, way],
            ring_s.at[0, p, way],
            ring_r.at[0, p, way],
            col=(right, left)[way],
        )

    def copy_b(p, way):
        return remote(
            send_b.at[p, way],
            recv_b.at[p, way],
            ring_s.at[1, p, way],
            ring_r.at[1, p, way],
            col=(right, left)[way],
        )

    def copy_g(p, way, slot):
        return remote(
            s.at[p, slot],
            s.at[p, slot],
            ring_s.at[2, p, way],
            ring_r.at[2, p, way],
            col=(right, left)[way],
        )

    def copy_f(p, way, slot):
        rows = pl.ds(way * half, half)
        return remote(
            s.at[p, slot, rows],
            s.at[p, slot, rows],
            ring_s.at[3, p, way],
            ring_r.at[3, p, way],
            col=(right, left)[way],
        )

    copy_a(0, 0).start()
    copy_a(0, 1).start()

    def gate_step(p, carry):
        x_load(p).wait()
        gate_term(p)
        copy_a(p, 0).start()
        copy_a(p, 1).start()
        return carry

    lax.fori_loop(1, nq, gate_step, 0)

    slab = ends_part.shape[0]
    loads["og"].wait()
    loads["pdo"].wait()
    loads["pui"].wait()
    pdo[pl.ds(k_dim, k_dim)] = jnp.zeros((k_dim, pdo.shape[1]), bf16)
    pui[pl.ds(0, k_dim)] = jnp.zeros((k_dim, pui.shape[1]), bf16)
    mine = pl.ds(pl.multiple_of((upper_y * n_z + z) * slab, slab), slab)
    ends_part[...] = (dot_nt(og[mine], pdo[...]) + dot_nt(x[mine], pui[...])).astype(bf16)

    def copy_ends(k):
        return remote(
            ends_part,
            ends_recv.at[k - 1],
            ends_s.at[k - 1],
            ends_r.at[k - 1],
            col=lax.rem(c + k, n_col),
        )

    for k in range(1, n_col):
        copy_ends(k).start()

    loads["wu"].wait()
    loads["wd"].wait()

    def terms_step(p, carry):
        up[p] = dot(x[token_rows(p)], wu[...]).astype(bf16)
        copy_a(p, 0).wait_recv()
        send_b[p, 0, pl.ds(0, half)] = (
            gate[p, own_rows(right, 0, half)] + recv_a[p, 0].astype(f32)
        ).astype(bf16)
        send_b[p, 0, pl.ds(half, half)] = gate[p, own_rows(right, half, half)].astype(bf16)
        copy_b(p, 0).start()
        copy_a(p, 1).wait_recv()
        send_b[p, 1, pl.ds(0, half)] = gate[p, own_rows(left, 0, half)].astype(bf16)
        send_b[p, 1, pl.ds(half, half)] = (
            gate[p, own_rows(left, half, half)] + recv_a[p, 1].astype(f32)
        ).astype(bf16)
        copy_b(p, 1).start()
        hg[p] = dot_nt(og[token_rows(p)], wd[...]).astype(bf16)
        return carry

    lax.fori_loop(0, nq, terms_step, 0)

    for k in range(1, n_col):
        copy_ends(k).wait_recv()
    total = ends_part[...].astype(f32)
    for k in range(1, n_col):
        total += ends_recv[k - 1].astype(f32)
    ends[mine] = total.astype(bf16)

    def copy_gather(k, owner):
        rows = pl.ds(pl.multiple_of((upper_y * n_z + owner) * slab, slab), slab)
        return remote(
            ends.at[rows],
            ends.at[rows],
            gather_s.at[k - 1],
            gather_r.at[k - 1],
            **along_z(k),
        )

    def copy_pair(owner):
        rows = pl.ds(pl.multiple_of(owner * n_z * slab, n_z * slab), n_z * slab)
        return remote(ends.at[rows], ends.at[rows], pair_s, pair_r, **along_y(0, 1))

    for k in range(1, n_z):
        copy_gather(k, z).start()

    loads["store"].wait()
    squares = jnp.zeros((store.shape[0], LANES), f32)
    for j in range(store.shape[1] // LANES):
        value = store[:, pl.ds(j * LANES, LANES)].astype(f32)
        squares += value * value
    upper = squares.astype(bf16)
    lower = (squares - upper.astype(f32)).astype(bf16)
    ones = jnp.ones((8, LANES), bf16)
    doc_squares = dot_nt(ones, upper) + dot_nt(ones, lower)
    loads["mask"].wait()
    keep = jnp.where(c < n_col // 2, mask[0:1, :], mask[1:2, :]).astype(f32)
    doc_squares = doc_squares * keep
    out_width = store.shape[0] // n_col
    for j in range(n_col):
        norm_send[j] = doc_squares[:, j * out_width : (j + 1) * out_width]

    def copy_norm(k):
        to = lax.rem(c + k, n_col)
        return remote(
            norm_send.at[to], norm_recv.at[k - 1], norm_s.at[k - 1], norm_r.at[k - 1], col=to
        )

    def own_step(p, carry):
        copy_b(p, 0).wait_recv()
        copy_b(p, 1).wait_recv()
        value = (
            gate[p, own_rows(c, 0, part)] + recv_b[p, 0].astype(f32) + recv_b[p, 1].astype(f32)
        )
        s[p, c] = (value * jax.nn.sigmoid(value)).astype(bf16)
        copy_g(p, 0, c).start()
        copy_g(p, 1, c).start()
        return carry

    def forward_step(p, carry):
        copy_g(p, 0, left).wait_recv()
        copy_f(p, 0, left).start()
        copy_g(p, 1, right).wait_recv()
        copy_f(p, 1, right).start()
        return carry

    lax.fori_loop(0, early, own_step, 0)
    for k in range(1, n_col):
        copy_norm(k).start()

    n_query = n_grp * nq
    n_sub = x_recv.shape[2]
    for k in range(1, n_z):
        copy_gather(k, lax.rem(z + n_z - k, n_z)).wait_recv()
    copy_pair(upper_y).start()
    lax.fori_loop(0, early - 1, forward_step, 0)
    copy_pair(1 - upper_y).wait_recv()
    low_lanes = lax.broadcasted_iota(jnp.int32, (SEQ, LANES), 1) < k_dim

    def ends_step(p, carry):
        value = ends[token_rows(p)].astype(f32)
        ends_t[p] = value.T[:k_dim].astype(bf16)
        ui2[p] = jnp.where(low_lanes, pltpu.roll(value, k_dim, 1), value).astype(bf16)
        return carry

    lax.fori_loop(0, nq, ends_step, 0)

    lax.fori_loop(early, early + 1, own_step, 0)
    lax.fori_loop(early - 1, early, forward_step, 0)
    lax.fori_loop(early + 1, nq, own_step, 0)

    loads["pdi"].wait()
    loads["pdi2"].wait()
    loads["puo"].wait()
    low_half = lax.broadcasted_iota(jnp.int32, (k_dim // 2, LANES), 1) < k_dim

    def grads_step(p, carry):
        copy_f(p, 0, across).wait_recv()
        copy_f(p, 1, across).wait_recv()
        shared = s[p].reshape(SEQ, s.shape[-1])
        down_in = dot_nt(up[p] * shared, pdi[...])
        up_out = dot_nt(puo[...], hg[p] * shared)
        pairs[pl.ds(0, k_dim)] = dot(ends_t[p], down_in.astype(bf16))
        pairs[pl.ds(k_dim, k_dim)] = dot(up_out.astype(bf16), ui2[p])
        for m in range(2):
            even = pairs[pl.ds(m * k_dim, k_dim // 2, 2)]
            odd = pairs[pl.ds(m * k_dim + 1, k_dim // 2, 2)]
            value = jnp.where(low_half, even, odd)
            grads[p, pl.ds(m * (k_dim // 2), k_dim // 2)] = value
            grads_send[p, pl.ds(m * (k_dim // 2), k_dim // 2)] = value.astype(bf16)
        return carry

    def copy_x(batch, k):
        first, count = batches[batch]
        to = lax.rem(c + k, n_col)
        return remote(
            grads_send.at[
                pl.ds(first, count), pl.ds(pl.multiple_of(to * n_sub, n_sub), n_sub)
            ],
            x_recv.at[k - 1, pl.ds(first, count)],
            x_s.at[batch, k - 1],
            x_r.at[batch, k - 1],
            col=to,
        )

    def copy_z(batch, k):
        first, count = batches[batch]
        return remote(
            block_send.at[pl.ds(first, count)],
            z_recv.at[k - 1, pl.ds(first, count)],
            z_s.at[batch, k - 1],
            z_r.at[batch, k - 1],
            **along_z(k),
        )

    def copy_y(batch, j, e):
        first, count = batches[batch]
        return remote(
            y_send.at[pl.ds(first, count)],
            y_recv.at[j, e, pl.ds(first, count)],
            y_s.at[batch, j, e],
            y_r.at[batch, j, e],
            **along_y(j, e),
        )

    def make_grads(batch):
        first, count = batches[batch]
        lax.fori_loop(first, first + count, grads_step, 0)
        for k in x_steps:
            copy_x(batch, k).start()

    def sum_col(batch):
        first, count = batches[batch]
        span = pl.ds(first, count)
        for k in range(1, n_col):
            copy_x(batch, k).wait_recv()
        total = grads[span, pl.ds(pl.multiple_of(c * n_sub, n_sub), n_sub)]
        for k in range(1, n_col):
            total += x_recv[k - 1, span].astype(f32)
        block[span] = total
        block_send[span] = total.astype(bf16)

        for k in z_steps:
            copy_z(batch, k).start()

    def sum_z(batch):
        first, count = batches[batch]
        span = pl.ds(first, count)

        for k in range(1, n_z):
            copy_z(batch, k).wait_recv()
        total = block[span]
        for k in range(1, n_z):
            total += z_recv[k - 1, span].astype(f32)
        block[span] = total
        y_send[span] = total.astype(bf16)
        for j, e in y_steps:
            copy_y(batch, j, e).start()

    def sum_y(batch):
        first, count = batches[batch]
        span = pl.ds(first, count)
        for j in range(n_grp):
            copy_y(batch, j, 1).wait_recv()
            if j:
                copy_y(batch, j, 0).wait_recv()
                total = y_recv[j, 0, span].astype(f32)
            else:
                total = block[span]
            total += y_recv[j, 1, span].astype(f32)
            for q in range(count):
                row = lax.rem(g + n_grp - j, n_grp) * nq + first + q
                full[pl.ds(row, n_sub, n_query), :] = total[q]

    make_grads(0)
    lax.fori_loop(early, nq, forward_step, 0)
    sum_col(0)
    make_grads(1)
    make_grads(2)
    sum_col(1)
    sum_z(0)
    sum_col(2)
    sum_z(1)
    sum_y(0)
    sum_z(2)
    sum_y(1)
    sum_y(2)

    query = jnp.concatenate(
        [full[pl.ds(kk * n_query, n_query), :] for kk in range(n_sub)], axis=1
    )
    raw = dot_nt(query.astype(bf16), store[...]) * keep
    query_squares = jnp.broadcast_to(
        jnp.sum(query * query, axis=1, keepdims=True), (n_query, out_width)
    )
    for j in range(n_col):
        c_send[j] = jnp.concatenate(
            [raw[:, j * out_width : (j + 1) * out_width], query_squares], axis=0
        ).astype(bf16)

    def copy_c(k):
        to = lax.rem(c + k, n_col)
        return remote(c_send.at[to], c_recv.at[k - 1], c_s.at[k - 1], c_r.at[k - 1], col=to)

    for k in x_steps:
        copy_c(k).start()
    def ring_done(p, carry):
        for way in range(2):
            copy_a(p, way).wait_send()
            copy_b(p, way).wait_send()
            copy_g(p, way, c).wait_send()
            copy_f(p, way, left).wait_send()
        return carry

    lax.fori_loop(0, nq, ring_done, 0)

    for k in range(1, n_z):
        copy_gather(k, z).wait_send()
        for batch in range(len(batches)):
            copy_z(batch, k).wait_send()
    copy_pair(upper_y).wait_send()
    for k in range(1, n_col):
        copy_ends(k).wait_send()
        copy_norm(k).wait_send()
        for batch in range(len(batches)):
            copy_x(batch, k).wait_send()
    for j, e in y_steps:
        for batch in range(len(batches)):
            copy_y(batch, j, e).wait_send()
    norms = norm_send[c]
    for k in range(1, n_col):
        copy_norm(k).wait_recv()
        norms += norm_recv[k - 1]
    columns = float(n_col * n_sub * LANES)
    doc_norm = jnp.sqrt(norms[0:1] / columns + EPSILON) * math.sqrt(columns)
    total = c_send[c].astype(f32)
    for k in range(1, n_col):
        copy_c(k).wait_recv()
    for k in range(1, n_col):
        total += c_recv[k - 1].astype(f32)
    query_norm = jnp.sqrt(total[n_query:] / columns + EPSILON)
    scores = total[:n_query] / (query_norm * doc_norm)
    slot = c * out_width + lax.broadcasted_iota(jnp.int32, scores.shape, 1)
    loads["live"].wait()
    out_ref[...] = jnp.where(slot < live[0], scores, 0.0)
    for k in x_steps:
        copy_c(k).wait_send()


def local(
    mlp_input,
    out_grad,
    w_gate,
    w_up,
    w_down,
    proj_down_in,
    proj_down_out,
    proj_up_in,
    proj_up_out,
    store,
    layer_mask,
    live_count,
):
    n_grp, n_doc, n_col = (lax.axis_size(name) for name in ("grp", "doc", "col"))
    tokens, depth = mlp_input.shape
    width = w_gate.shape[1]
    k_dim = proj_down_in.shape[1]
    nq = tokens // SEQ
    part = SEQ // n_col
    slab = tokens // n_doc
    n_row = 2 * k_dim * k_dim // LANES
    n_sub = n_row // n_col
    out_width = store.shape[0] // n_col
    dma = pltpu.SemaphoreType.DMA
    scratch = [
        pltpu.VMEM((tokens, depth), bf16),
        pltpu.VMEM((tokens, depth), bf16),
        pltpu.VMEM((depth, width), bf16),
        pltpu.VMEM((depth, width), bf16),
        pltpu.VMEM((width, depth), bf16),
        pltpu.VMEM((2 * k_dim, width), bf16),
        pltpu.VMEM((2 * k_dim, depth), bf16),
        pltpu.VMEM((2 * k_dim, depth), bf16),
        pltpu.VMEM((k_dim, width), bf16),
        pltpu.VMEM(store.shape, bf16),
        pltpu.VMEM(layer_mask.shape[::-1], jnp.int32),
        pltpu.SMEM(live_count.shape, jnp.int32),
        pltpu.VMEM((nq, SEQ, width), f32),
        pltpu.VMEM((nq, SEQ, width), bf16),
        pltpu.VMEM((nq, SEQ, width), bf16),
        pltpu.VMEM((nq, n_col, part, width), bf16),
        pltpu.VMEM((nq, part, width), bf16),
        pltpu.VMEM((nq, 2, part // 2, width), bf16),
        pltpu.VMEM((nq, 2, part, width), bf16),
        pltpu.VMEM((nq, 2, part, width), bf16),
        pltpu.VMEM((slab, LANES), bf16),
        pltpu.VMEM((n_col - 1, slab, LANES), bf16),
        pltpu.VMEM((tokens, LANES), bf16),
        pltpu.VMEM((nq, k_dim, SEQ), bf16),
        pltpu.VMEM((nq, SEQ, LANES), bf16),
        pltpu.VMEM((2 * k_dim, LANES), f32),
        pltpu.VMEM((nq, n_row, LANES), f32),
        pltpu.VMEM((nq, n_row, LANES), bf16),
        pltpu.VMEM((n_col - 1, nq, n_sub, LANES), bf16),
        pltpu.VMEM((nq, n_sub, LANES), f32),
        pltpu.VMEM((nq, n_sub, LANES), bf16),
        pltpu.VMEM((n_doc // 2 - 1, nq, n_sub, LANES), bf16),
        pltpu.VMEM((nq, n_sub, LANES), bf16),
        pltpu.VMEM((n_grp, 2, nq, n_sub, LANES), bf16),
        pltpu.VMEM((n_sub * n_grp * nq, LANES), f32),
        pltpu.VMEM((n_col, 8, out_width), f32),
        pltpu.VMEM((n_col - 1, 8, out_width), f32),
        pltpu.VMEM((n_col, 2 * n_grp * nq, out_width), bf16),
        pltpu.VMEM((n_col - 1, 2 * n_grp * nq, out_width), bf16),
        dma((12,)),
        dma((nq,)),
        dma((4, nq, 2)),
        dma((4, nq, 2)),
        dma((n_col - 1,)),
        dma((n_col - 1,)),
        dma((n_doc // 2 - 1,)),
        dma((n_doc // 2 - 1,)),
        dma(()),
        dma(()),
        dma((3, n_col - 1)),
        dma((3, n_col - 1)),
        dma((3, n_doc // 2 - 1)),
        dma((3, n_doc // 2 - 1)),
        dma((3, n_grp, 2)),
        dma((3, n_grp, 2)),
        dma((n_col - 1,)),
        dma((n_col - 1,)),
        dma((n_col - 1,)),
        dma((n_col - 1,)),
    ]
    scores = pl.pallas_call(
        functools.partial(kernel, (n_grp, n_doc, n_col, nq)),
        out_shape=jax.ShapeDtypeStruct((n_grp * nq, out_width), f32),
        in_specs=[pl.BlockSpec(memory_space=pl.ANY)] * 12,
        out_specs=pl.BlockSpec(memory_space=pltpu.VMEM),
        scratch_shapes=scratch,
        compiler_params=pltpu.CompilerParams(
            collective_id=0, has_side_effects=True, vmem_limit_bytes=58 * 1024 * 1024
        ),
        cost_estimate=pl.CostEstimate(
            flops=6 * tokens * depth * width, bytes_accessed=14 << 20, transcendentals=0
        ),
    )(
        mlp_input,
        out_grad,
        w_gate,
        w_up,
        w_down,
        proj_down_in.T,
        proj_down_out.T,
        proj_up_in.T,
        proj_up_out.T,
        store,
        layer_mask.T,
        live_count,
    )
    return scores


def solution(mesh):
    return jax.shard_map(
        local,
        mesh=mesh,
        in_specs=(
            P("grp", "col"),
            P("grp", "col"),
            P("col", "doc"),
            P("col", "doc"),
            P("doc", "col"),
            P("doc", None),
            P("col", None),
            P("col", None),
            P("doc", None),
            P(("grp", "doc"), "col"),
            P(("grp", "doc"), None),
            P(("grp", "doc")),
        ),
        out_specs=P(None, ("grp", "doc", "col")),
        check_vma=False,
    )
```

```python
import functools
import math

import jax
import jax.numpy as jnp
from jax import lax
from jax.experimental import pallas as pl
from jax.experimental.pallas import tpu as pltpu
from jax.sharding import PartitionSpec as P

MESH = pl.DeviceIdType.MESH
SEQ = 256
LANES = 128
EPSILON = 1e-06
NT = (((1,), (1,)), ((), ()))
f32, bf16 = jnp.float32, jnp.bfloat16


def dot(left, right):
    return jnp.dot(left, right, preferred_element_type=f32)


def dot_nt(left, right):
    return lax.dot_general(left, right, NT, preferred_element_type=f32)


def kernel(
    sizes,
    x_in,
    og_in,
    wg_in,
    wu_in,
    wd_in,
    pdi_in,
    pdo_in,
    pui_in,
    puo_in,
    store_in,
    mask_in,
    live_in,
    out_ref,
    x,
    og,
    wg,
    wu,
    wd,
    pdi,
    pdo,
    pui,
    puo,
    store,
    mask,
    live,
    gate,
    up,
    hg,
    s,
    send_a,
    recv_a,
    send_b,
    recv_b,
    ends_part,
    ends_recv,
    ends,
    ends_t,
    ui2,
    pairs,
    grads,
    grads_send,
    x_recv,
    block,
    block_send,
    z_recv,
    y_send,
    y_recv,
    full,
    norm_send,
    norm_recv,
    c_send,
    c_recv,
    load_sem,
    x_load_sem,
    ring_s,
    ring_r,
    ends_s,
    ends_r,
    gather_s,
    gather_r,
    pair_s,
    pair_r,
    x_s,
    x_r,
    z_s,
    z_r,
    y_s,
    y_r,
    norm_s,
    norm_r,
    c_s,
    c_r,
):
    n_grp, n_doc, n_col, nq = sizes
    part = SEQ // n_col
    half = part // 2
    early = nq // 2
    batches = ((0, early), (early, nq - 1 - early), (nq - 1, 1))
    g, d, c = lax.axis_index("grp"), lax.axis_index("doc"), lax.axis_index("col")
    right, left, across = (
        lax.rem(c + 1, n_col),
        lax.rem(c + n_col - 1, n_col),
        lax.rem(c + 2, n_col),
    )
    n_z = n_doc // 2
    z, upper_y = d // 2, lax.rem(d, 2)
    k_dim = pdi_in.shape[0]

    def along_z(k):
        return {"doc": lax.rem(z + k, n_z) * 2 + upper_y}

    def along_y(j, e):
        return {"grp": lax.rem(g + j, n_grp), "doc": z * 2 + (upper_y + e - 2 * upper_y * e)}

    x_steps = sorted(range(1, n_col), key=lambda k: -min(k, n_col - k))
    z_steps = sorted(range(1, n_z), key=lambda k: -min(k, n_z - k))
    y_steps = [(j, e) for e in (1, 0) for j in range(n_grp) if j or e]

    def remote(src, dst, send, recv, **place):
        return pltpu.make_async_remote_copy(
            src_ref=src,
            dst_ref=dst,
            send_sem=send,
            recv_sem=recv,
            device_id=place,
            device_id_type=MESH,
        )

    def token_rows(p):
        return pl.ds(pl.multiple_of(p * SEQ, SEQ), SEQ)

    def own_rows(owner, first, count):
        return pl.ds(pl.multiple_of(owner * part + first, half), count)

    loads = {}

    def load(key, src, dst):
        copy = pltpu.make_async_copy(src, dst, load_sem.at[len(loads)])
        copy.start()
        loads[key] = copy

    def x_load(p):
        return pltpu.make_async_copy(
            x_in.at[token_rows(p)], x.at[token_rows(p)], x_load_sem.at[p]
        )

    load("wg", wg_in, wg)
    x_load(0).start()

    barrier = pltpu.get_barrier_semaphore()

    def greet(place):
        pl.semaphore_signal(barrier, 1, device_id=place, device_id_type=MESH)

    for k in z_steps:
        greet(along_z(k))
    for j, e in y_steps:
        greet(along_y(j, e))
    for k in x_steps:
        greet({"col": lax.rem(c + k, n_col)})
    for p in range(1, nq):
        x_load(p).start()

    loads["wg"].wait()
    x_load(0).wait()
    load("og", og_in, og)
    load("pdo", pdo_in, pdo.at[pl.ds(0, k_dim)])
    load("pui", pui_in, pui.at[pl.ds(k_dim, k_dim)])
    load("wu", wu_in, wu)
    load("wd", wd_in, wd)
    load("store", store_in, store)
    load("mask", mask_in, mask)
    load("pdi", pdi_in, pdi.at[pl.ds(0, k_dim)])
    load("pdi2", pdi_in, pdi.at[pl.ds(k_dim, k_dim)])
    load("puo", puo_in, puo)
    load("live", live_in, live)

    def gate_term(p):
        gate[p] = dot(x[token_rows(p)], wg[...])
        send_a[p] = gate[p, own_rows(across, 0, part)].astype(bf16)

    gate_term(0)
    pl.semaphore_wait(barrier, n_z - 1 + len(y_steps) + n_col - 1)

    def copy_a(p, way):
        rows = pl.ds(way * half, half)
        return remote(
            send_a.at[p, rows],
            recv_a.at[p, way],
            ring_s.at[0, p, way],
            ring_r.at[0, p, way],
            col=(right, left)[way],
        )

    def copy_b(p, way):
        return remote(
            send_b.at[p, way],
            recv_b.at[p, way],
            ring_s.at[1, p, way],
            ring_r.at[1, p, way],
            col=(right, left)[way],
        )

    def copy_g(p, way, slot):
        return remote(
            s.at[p, slot],
            s.at[p, slot],
            ring_s.at[2, p, way],
            ring_r.at[2, p, way],
            col=(right, left)[way],
        )

    def copy_f(p, way, slot):
        rows = pl.ds(way * half, half)
        return remote(
            s.at[p, slot, rows],
            s.at[p, slot, rows],
            ring_s.at[3, p, way],
            ring_r.at[3, p, way],
            col=(right, left)[way],
        )

    copy_a(0, 0).start()
    copy_a(0, 1).start()

    def gate_step(p, carry):
        x_load(p).wait()
        gate_term(p)
        copy_a(p, 0).start()
        copy_a(p, 1).start()
        return carry

    lax.fori_loop(1, nq, gate_step, 0)

    slab = ends_part.shape[0]
    loads["og"].wait()
    loads["pdo"].wait()
    loads["pui"].wait()
    pdo[pl.ds(k_dim, k_dim)] = jnp.zeros((k_dim, pdo.shape[1]), bf16)
    pui[pl.ds(0, k_dim)] = jnp.zeros((k_dim, pui.shape[1]), bf16)
    mine = pl.ds(pl.multiple_of((upper_y * n_z + z) * slab, slab), slab)
    ends_part[...] = (dot_nt(og[mine], pdo[...]) + dot_nt(x[mine], pui[...])).astype(bf16)

    def copy_ends(k):
        return remote(
            ends_part,
            ends_recv.at[k - 1],
            ends_s.at[k - 1],
            ends_r.at[k - 1],
            col=lax.rem(c + k, n_col),
        )

    for k in range(1, n_col):
        copy_ends(k).start()

    loads["wu"].wait()
    loads["wd"].wait()

    def terms_step(p, carry):
        up[p] = dot(x[token_rows(p)], wu[...]).astype(bf16)
        copy_a(p, 0).wait_recv()
        send_b[p, 0, pl.ds(0, half)] = (
            gate[p, own_rows(right, 0, half)] + recv_a[p, 0].astype(f32)
        ).astype(bf16)
        send_b[p, 0, pl.ds(half, half)] = gate[p, own_rows(right, half, half)].astype(bf16)
        copy_b(p, 0).start()
        copy_a(p, 1).wait_recv()
        send_b[p, 1, pl.ds(0, half)] = gate[p, own_rows(left, 0, half)].astype(bf16)
        send_b[p, 1, pl.ds(half, half)] = (
            gate[p, own_rows(left, half, half)] + recv_a[p, 1].astype(f32)
        ).astype(bf16)
        copy_b(p, 1).start()
        hg[p] = dot_nt(og[token_rows(p)], wd[...]).astype(bf16)
        return carry

    lax.fori_loop(0, nq, terms_step, 0)

    for k in range(1, n_col):
        copy_ends(k).wait_recv()
    total = ends_part[...].astype(f32)
    for k in range(1, n_col):
        total += ends_recv[k - 1].astype(f32)
    ends[mine] = total.astype(bf16)

    def copy_gather(k, owner):
        rows = pl.ds(pl.multiple_of((upper_y * n_z + owner) * slab, slab), slab)
        return remote(
            ends.at[rows],
            ends.at[rows],
            gather_s.at[k - 1],
            gather_r.at[k - 1],
            **along_z(k),
        )

    def copy_pair(owner):
        rows = pl.ds(pl.multiple_of(owner * n_z * slab, n_z * slab), n_z * slab)
        return remote(ends.at[rows], ends.at[rows], pair_s, pair_r, **along_y(0, 1))

    for k in range(1, n_z):
        copy_gather(k, z).start()

    loads["store"].wait()
    squares = jnp.zeros((store.shape[0], LANES), f32)
    for j in range(store.shape[1] // LANES):
        value = store[:, pl.ds(j * LANES, LANES)].astype(f32)
        squares += value * value
    upper = squares.astype(bf16)
    lower = (squares - upper.astype(f32)).astype(bf16)
    ones = jnp.ones((8, LANES), bf16)
    doc_squares = dot_nt(ones, upper) + dot_nt(ones, lower)
    loads["mask"].wait()
    keep = jnp.where(c < n_col // 2, mask[0:1, :], mask[1:2, :]).astype(f32)
    doc_squares = doc_squares * keep
    out_width = store.shape[0] // n_col
    for j in range(n_col):
        norm_send[j] = doc_squares[:, j * out_width : (j + 1) * out_width]

    def copy_norm(k):
        to = lax.rem(c + k, n_col)
        return remote(
            norm_send.at[to], norm_recv.at[k - 1], norm_s.at[k - 1], norm_r.at[k - 1], col=to
        )

    def own_step(p, carry):
        copy_b(p, 0).wait_recv()
        copy_b(p, 1).wait_recv()
        value = (
            gate[p, own_rows(c, 0, part)] + recv_b[p, 0].astype(f32) + recv_b[p, 1].astype(f32)
        )
        s[p, c] = (value * jax.nn.sigmoid(value)).astype(bf16)
        copy_g(p, 0, c).start()
        copy_g(p, 1, c).start()
        return carry

    def forward_step(p, carry):
        copy_g(p, 0, left).wait_recv()
        copy_f(p, 0, left).start()
        copy_g(p, 1, right).wait_recv()
        copy_f(p, 1, right).start()
        return carry

    lax.fori_loop(0, early, own_step, 0)
    for k in range(1, n_col):
        copy_norm(k).start()

    n_query = n_grp * nq
    n_sub = x_recv.shape[2]
    for k in range(1, n_z):
        copy_gather(k, lax.rem(z + n_z - k, n_z)).wait_recv()
    copy_pair(upper_y).start()
    lax.fori_loop(0, early - 1, forward_step, 0)
    copy_pair(1 - upper_y).wait_recv()
    low_lanes = lax.broadcasted_iota(jnp.int32, (SEQ, LANES), 1) < k_dim

    def ends_step(p, carry):
        value = ends[token_rows(p)].astype(f32)
        ends_t[p] = value.T[:k_dim].astype(bf16)
        ui2[p] = jnp.where(low_lanes, pltpu.roll(value, k_dim, 1), value).astype(bf16)
        return carry

    lax.fori_loop(0, nq, ends_step, 0)

    lax.fori_loop(early, early + 1, own_step, 0)
    lax.fori_loop(early - 1, early, forward_step, 0)
    lax.fori_loop(early + 1, nq, own_step, 0)

    loads["pdi"].wait()
    loads["pdi2"].wait()
    loads["puo"].wait()
    low_half = lax.broadcasted_iota(jnp.int32, (k_dim // 2, LANES), 1) < k_dim

    def grads_step(p, carry):
        copy_f(p, 0, across).wait_recv()
        copy_f(p, 1, across).wait_recv()
        shared = s[p].reshape(SEQ, s.shape[-1])
        down_in = dot_nt(up[p] * shared, pdi[...])
        up_out = dot_nt(puo[...], hg[p] * shared)
        pairs[pl.ds(0, k_dim)] = dot(ends_t[p], down_in.astype(bf16))
        pairs[pl.ds(k_dim, k_dim)] = dot(up_out.astype(bf16), ui2[p])
        for m in range(2):
            even = pairs[pl.ds(m * k_dim, k_dim // 2, 2)]
            odd = pairs[pl.ds(m * k_dim + 1, k_dim // 2, 2)]
            value = jnp.where(low_half, even, odd)
            grads[p, pl.ds(m * (k_dim // 2), k_dim // 2)] = value
            grads_send[p, pl.ds(m * (k_dim // 2), k_dim // 2)] = value.astype(bf16)
        return carry

    def copy_x(batch, k):
        first, count = batches[batch]
        to = lax.rem(c + k, n_col)
        return remote(
            grads_send.at[
                pl.ds(first, count), pl.ds(pl.multiple_of(to * n_sub, n_sub), n_sub)
            ],
            x_recv.at[k - 1, pl.ds(first, count)],
            x_s.at[batch, k - 1],
            x_r.at[batch, k - 1],
            col=to,
        )

    def copy_z(batch, k):
        first, count = batches[batch]
        return remote(
            block_send.at[pl.ds(first, count)],
            z_recv.at[k - 1, pl.ds(first, count)],
            z_s.at[batch, k - 1],
            z_r.at[batch, k - 1],
            **along_z(k),
        )

    def copy_y(batch, j, e):
        first, count = batches[batch]
        return remote(
            y_send.at[pl.ds(first, count)],
            y_recv.at[j, e, pl.ds(first, count)],
            y_s.at[batch, j, e],
            y_r.at[batch, j, e],
            **along_y(j, e),
        )

    def make_grads(batch):
        first, count = batches[batch]
        lax.fori_loop(first, first + count, grads_step, 0)
        for k in x_steps:
            copy_x(batch, k).start()

    def sum_col(batch):
        first, count = batches[batch]
        span = pl.ds(first, count)
        for k in range(1, n_col):
            copy_x(batch, k).wait_recv()
        total = grads[span, pl.ds(pl.multiple_of(c * n_sub, n_sub), n_sub)]
        for k in range(1, n_col):
            total += x_recv[k - 1, span].astype(f32)
        block[span] = total
        block_send[span] = total.astype(bf16)

        for k in z_steps:
            copy_z(batch, k).start()

    def sum_z(batch):
        first, count = batches[batch]
        span = pl.ds(first, count)

        for k in range(1, n_z):
            copy_z(batch, k).wait_recv()
        total = block[span]
        for k in range(1, n_z):
            total += z_recv[k - 1, span].astype(f32)
        block[span] = total
        y_send[span] = total.astype(bf16)
        for j, e in y_steps:
            copy_y(batch, j, e).start()

    def sum_y(batch):
        first, count = batches[batch]
        span = pl.ds(first, count)
        for j in range(n_grp):
            copy_y(batch, j, 1).wait_recv()
            if j:
                copy_y(batch, j, 0).wait_recv()
                total = y_recv[j, 0, span].astype(f32)
            else:
                total = block[span]
            total += y_recv[j, 1, span].astype(f32)
            for q in range(count):
                row = lax.rem(g + n_grp - j, n_grp) * nq + first + q
                full[pl.ds(row, n_sub, n_query), :] = total[q]

    make_grads(0)
    lax.fori_loop(early, nq, forward_step, 0)
    sum_col(0)
    make_grads(1)
    make_grads(2)
    sum_col(1)
    sum_z(0)
    sum_col(2)
    sum_z(1)
    sum_y(0)
    sum_z(2)
    sum_y(1)
    sum_y(2)

    query = jnp.concatenate(
        [full[pl.ds(kk * n_query, n_query), :] for kk in range(n_sub)], axis=1
    )
    raw = dot_nt(query.astype(bf16), store[...]) * keep
    query_squares = jnp.broadcast_to(
        jnp.sum(query * query, axis=1, keepdims=True), (n_query, out_width)
    )
    for j in range(n_col):
        c_send[j] = jnp.concatenate(
            [raw[:, j * out_width : (j + 1) * out_width], query_squares], axis=0
        ).astype(bf16)

    def copy_c(k):
        to = lax.rem(c + k, n_col)
        return remote(c_send.at[to], c_recv.at[k - 1], c_s.at[k - 1], c_r.at[k - 1], col=to)

    for k in x_steps:
        copy_c(k).start()
    def ring_done(p, carry):
        for way in range(2):
            copy_a(p, way).wait_send()
            copy_b(p, way).wait_send()
            copy_g(p, way, c).wait_send()
            copy_f(p, way, left).wait_send()
        return carry

    lax.fori_loop(0, nq, ring_done, 0)

    for k in range(1, n_z):
        copy_gather(k, z).wait_send()
        for batch in range(len(batches)):
            copy_z(batch, k).wait_send()
    copy_pair(upper_y).wait_send()
    for k in range(1, n_col):
        copy_ends(k).wait_send()
        copy_norm(k).wait_send()
        for batch in range(len(batches)):
            copy_x(batch, k).wait_send()
    for j, e in y_steps:
        for batch in range(len(batches)):
            copy_y(batch, j, e).wait_send()
    norms = norm_send[c]
    for k in range(1, n_col):
        copy_norm(k).wait_recv()
        norms += norm_recv[k - 1]
    columns = float(n_col * n_sub * LANES)
    doc_norm = jnp.sqrt(norms[0:1] / columns + EPSILON) * math.sqrt(columns)
    total = c_send[c].astype(f32)
    for k in range(1, n_col):
        copy_c(k).wait_recv()
    for k in range(1, n_col):
        total += c_recv[k - 1].astype(f32)
    query_norm = jnp.sqrt(total[n_query:] / columns + EPSILON)
    scores = total[:n_query] / (query_norm * doc_norm)
    slot = c * out_width + lax.broadcasted_iota(jnp.int32, scores.shape, 1)
    loads["live"].wait()
    out_ref[...] = jnp.where(slot < live[0], scores, 0.0)
    for k in x_steps:
        copy_c(k).wait_send()


def local(
    mlp_input,
    out_grad,
    w_gate,
    w_up,
    w_down,
    proj_down_in,
    proj_down_out,
    proj_up_in,
    proj_up_out,
    store,
    layer_mask,
    live_count,
):
    n_grp, n_doc, n_col = (lax.axis_size(name) for name in ("grp", "doc", "col"))
    tokens, depth = mlp_input.shape
    width = w_gate.shape[1]
    k_dim = proj_down_in.shape[1]
    nq = tokens // SEQ
    part = SEQ // n_col
    slab = tokens // n_doc
    n_row = 2 * k_dim * k_dim // LANES
    n_sub = n_row // n_col
    out_width = store.shape[0] // n_col
    dma = pltpu.SemaphoreType.DMA
    scratch = [
        pltpu.VMEM((tokens, depth), bf16),
        pltpu.VMEM((tokens, depth), bf16),
        pltpu.VMEM((depth, width), bf16),
        pltpu.VMEM((depth, width), bf16),
        pltpu.VMEM((width, depth), bf16),
        pltpu.VMEM((2 * k_dim, width), bf16),
        pltpu.VMEM((2 * k_dim, depth), bf16),
        pltpu.VMEM((2 * k_dim, depth), bf16),
        pltpu.VMEM((k_dim, width), bf16),
        pltpu.VMEM(store.shape, bf16),
        pltpu.VMEM(layer_mask.shape[::-1], jnp.int32),
        pltpu.SMEM(live_count.shape, jnp.int32),
        pltpu.VMEM((nq, SEQ, width), f32),
        pltpu.VMEM((nq, SEQ, width), bf16),
        pltpu.VMEM((nq, SEQ, width), bf16),
        pltpu.VMEM((nq, n_col, part, width), bf16),
        pltpu.VMEM((nq, part, width), bf16),
        pltpu.VMEM((nq, 2, part // 2, width), bf16),
        pltpu.VMEM((nq, 2, part, width), bf16),
        pltpu.VMEM((nq, 2, part, width), bf16),
        pltpu.VMEM((slab, LANES), bf16),
        pltpu.VMEM((n_col - 1, slab, LANES), bf16),
        pltpu.VMEM((tokens, LANES), bf16),
        pltpu.VMEM((nq, k_dim, SEQ), bf16),
        pltpu.VMEM((nq, SEQ, LANES), bf16),
        pltpu.VMEM((2 * k_dim + 8, LANES), f32),
        pltpu.VMEM((nq, n_row, LANES), f32),
        pltpu.VMEM((nq, n_row, LANES), bf16),
        pltpu.VMEM((n_col - 1, nq, n_sub, LANES), bf16),
        pltpu.VMEM((nq, n_sub, LANES), f32),
        pltpu.VMEM((nq, n_sub, LANES), bf16),
        pltpu.VMEM((n_doc // 2 - 1, nq, n_sub, LANES), bf16),
        pltpu.VMEM((nq, n_sub, LANES), bf16),
        pltpu.VMEM((n_grp, 2, nq, n_sub, LANES), bf16),
        pltpu.VMEM(((n_sub + 1) * n_grp * nq, LANES), f32),
        pltpu.VMEM((n_col, 8, out_width), f32),
        pltpu.VMEM((n_col - 1, 8, out_width), f32),
        pltpu.VMEM((n_col, 2 * n_grp * nq, out_width), bf16),
        pltpu.VMEM((n_col - 1, 2 * n_grp * nq, out_width), bf16),
        dma((12,)),
        dma((nq,)),
        dma((4, nq, 2)),
        dma((4, nq, 2)),
        dma((n_col - 1,)),
        dma((n_col - 1,)),
        dma((n_doc // 2 - 1,)),
        dma((n_doc // 2 - 1,)),
        dma(()),
        dma(()),
        dma((3, n_col - 1)),
        dma((3, n_col - 1)),
        dma((3, n_doc // 2 - 1)),
        dma((3, n_doc // 2 - 1)),
        dma((3, n_grp, 2)),
        dma((3, n_grp, 2)),
        dma((n_col - 1,)),
        dma((n_col - 1,)),
        dma((n_col - 1,)),
        dma((n_col - 1,)),
    ]
    scores = pl.pallas_call(
        functools.partial(kernel, (n_grp, n_doc, n_col, nq)),
        out_shape=jax.ShapeDtypeStruct((n_grp * nq, out_width), f32),
        in_specs=[pl.BlockSpec(memory_space=pl.ANY)] * 12,
        out_specs=pl.BlockSpec(memory_space=pltpu.VMEM),
        scratch_shapes=scratch,
        compiler_params=pltpu.CompilerParams(
            collective_id=0, has_side_effects=True, vmem_limit_bytes=58 * 1024 * 1024
        ),
        cost_estimate=pl.CostEstimate(
            flops=6 * tokens * depth * width, bytes_accessed=14 << 20, transcendentals=0
        ),
    )(
        mlp_input,
        out_grad,
        w_gate,
        w_up,
        w_down,
        proj_down_in.T,
        proj_down_out.T,
        proj_up_in.T,
        proj_up_out.T,
        store,
        layer_mask.T,
        live_count,
    )
    return scores


def solution(mesh):
    return jax.shard_map(
        local,
        mesh=mesh,
        in_specs=(
            P("grp", "col"),
            P("grp", "col"),
            P("col", "doc"),
            P("col", "doc"),
            P("doc", "col"),
            P("doc", None),
            P("col", None),
            P("col", None),
            P("doc", None),
            P(("grp", "doc"), "col"),
            P(("grp", "doc"), None),
            P(("grp", "doc")),
        ),
        out_specs=P(None, ("grp", "doc", "col")),
        check_vma=False,
    )
```

```python
import functools
import math

import jax
import jax.numpy as jnp
from jax import lax
from jax.experimental import pallas as pl
from jax.experimental.pallas import tpu as pltpu
from jax.sharding import PartitionSpec as P

MESH = pl.DeviceIdType.MESH
SEQ = 256
LANES = 128
EPSILON = 1e-06
NT = (((1,), (1,)), ((), ()))
f32, bf16 = jnp.float32, jnp.bfloat16


def dot(left, right):
    return jnp.dot(left, right, preferred_element_type=f32)


def dot_nt(left, right):
    return lax.dot_general(left, right, NT, preferred_element_type=f32)


def kernel(
    sizes,
    x_in,
    og_in,
    wg_in,
    wu_in,
    wd_in,
    pdi_in,
    pdo_in,
    pui_in,
    puo_in,
    store_in,
    mask_in,
    live_in,
    out_ref,
    x,
    og,
    wg,
    wu,
    wd,
    pdi,
    pdo,
    pui,
    puo,
    store,
    mask,
    live,
    gate,
    up,
    hg,
    s,
    send_a,
    recv_a,
    send_b,
    recv_b,
    ends_part,
    ends_recv,
    ends,
    ends_t,
    ui2,
    pairs,
    grads,
    grads_send,
    x_recv,
    block,
    block_send,
    z_recv,
    y_send,
    y_recv,
    full,
    norm_send,
    norm_recv,
    c_send,
    c_recv,
    load_sem,
    x_load_sem,
    ring_s,
    ring_r,
    ends_s,
    ends_r,
    gather_s,
    gather_r,
    pair_s,
    pair_r,
    x_s,
    x_r,
    z_s,
    z_r,
    y_s,
    y_r,
    norm_s,
    norm_r,
    c_s,
    c_r,
):
    n_grp, n_doc, n_col, nq = sizes
    part = SEQ // n_col
    half = part // 2
    early = nq // 2
    batches = ((0, early), (early, nq - 1 - early), (nq - 1, 1))
    g, d, c = lax.axis_index("grp"), lax.axis_index("doc"), lax.axis_index("col")
    right, left, across = (
        lax.rem(c + 1, n_col),
        lax.rem(c + n_col - 1, n_col),
        lax.rem(c + 2, n_col),
    )
    n_z = n_doc // 2
    z, upper_y = d // 2, lax.rem(d, 2)
    k_dim = pdi_in.shape[0]

    def along_z(k):
        return {"doc": lax.rem(z + k, n_z) * 2 + upper_y}

    def along_y(j, e):
        return {"grp": lax.rem(g + j, n_grp), "doc": z * 2 + (upper_y + e - 2 * upper_y * e)}

    x_steps = sorted(range(1, n_col), key=lambda k: -min(k, n_col - k))
    z_steps = sorted(range(1, n_z), key=lambda k: -min(k, n_z - k))
    y_steps = [(j, e) for e in (1, 0) for j in range(n_grp) if j or e]

    def remote(src, dst, send, recv, **place):
        return pltpu.make_async_remote_copy(
            src_ref=src,
            dst_ref=dst,
            send_sem=send,
            recv_sem=recv,
            device_id=place,
            device_id_type=MESH,
        )

    def token_rows(p):
        return pl.ds(pl.multiple_of(p * SEQ, SEQ), SEQ)

    def own_rows(owner, first, count):
        return pl.ds(pl.multiple_of(owner * part + first, half), count)

    loads = {}

    def load(key, src, dst):
        copy = pltpu.make_async_copy(src, dst, load_sem.at[len(loads)])
        copy.start()
        loads[key] = copy

    def x_load(p):
        return pltpu.make_async_copy(
            x_in.at[token_rows(p)], x.at[token_rows(p)], x_load_sem.at[p]
        )

    load("wg", wg_in, wg)
    x_load(0).start()

    barrier = pltpu.get_barrier_semaphore()

    def greet(place):
        pl.semaphore_signal(barrier, 1, device_id=place, device_id_type=MESH)

    for k in z_steps:
        greet(along_z(k))
    for j, e in y_steps:
        greet(along_y(j, e))
    for k in x_steps:
        greet({"col": lax.rem(c + k, n_col)})
    for p in range(1, nq):
        x_load(p).start()

    loads["wg"].wait()
    x_load(0).wait()
    load("og", og_in, og)
    load("pdo", pdo_in, pdo.at[pl.ds(0, k_dim)])
    load("pui", pui_in, pui.at[pl.ds(k_dim, k_dim)])
    load("wu", wu_in, wu)
    load("wd", wd_in, wd)
    load("store", store_in, store)
    load("mask", mask_in, mask)
    load("pdi", pdi_in, pdi.at[pl.ds(0, k_dim)])
    load("pdi2", pdi_in, pdi.at[pl.ds(k_dim, k_dim)])
    load("puo", puo_in, puo)
    load("live", live_in, live)

    def gate_term(p):
        gate[p] = dot(x[token_rows(p)], wg[...])
        send_a[p] = gate[p, own_rows(across, 0, part)].astype(bf16)

    first_rows = pl.ds(pl.multiple_of(across * part, part), part)
    send_a[0] = dot(x[first_rows], wg[...]).astype(bf16)
    pl.semaphore_wait(barrier, n_z - 1 + len(y_steps) + n_col - 1)

    def copy_a(p, way):
        rows = pl.ds(way * half, half)
        return remote(
            send_a.at[p, rows],
            recv_a.at[p, way],
            ring_s.at[0, p, way],
            ring_r.at[0, p, way],
            col=(right, left)[way],
        )

    def copy_b(p, way):
        return remote(
            send_b.at[p, way],
            recv_b.at[p, way],
            ring_s.at[1, p, way],
            ring_r.at[1, p, way],
            col=(right, left)[way],
        )

    def copy_g(p, way, slot):
        return remote(
            s.at[p, slot],
            s.at[p, slot],
            ring_s.at[2, p, way],
            ring_r.at[2, p, way],
            col=(right, left)[way],
        )

    def copy_f(p, way, slot):
        rows = pl.ds(way * half, half)
        return remote(
            s.at[p, slot, rows],
            s.at[p, slot, rows],
            ring_s.at[3, p, way],
            ring_r.at[3, p, way],
            col=(right, left)[way],
        )

    copy_a(0, 0).start()
    copy_a(0, 1).start()

    def gate_step(p, carry):
        x_load(p).wait()
        gate_term(p)
        copy_a(p, 0).start()
        copy_a(p, 1).start()
        return carry

    lax.fori_loop(1, nq, gate_step, 0)
    gate[0] = dot(x[token_rows(0)], wg[...])

    slab = ends_part.shape[0]
    loads["og"].wait()
    loads["pdo"].wait()
    loads["pui"].wait()
    pdo[pl.ds(k_dim, k_dim)] = jnp.zeros((k_dim, pdo.shape[1]), bf16)
    pui[pl.ds(0, k_dim)] = jnp.zeros((k_dim, pui.shape[1]), bf16)
    mine = pl.ds(pl.multiple_of((upper_y * n_z + z) * slab, slab), slab)
    ends_part[...] = (dot_nt(og[mine], pdo[...]) + dot_nt(x[mine], pui[...])).astype(bf16)

    def copy_ends(k):
        return remote(
            ends_part,
            ends_recv.at[k - 1],
            ends_s.at[k - 1],
            ends_r.at[k - 1],
            col=lax.rem(c + k, n_col),
        )

    for k in range(1, n_col):
        copy_ends(k).start()

    loads["wu"].wait()
    loads["wd"].wait()

    def terms_step(p, carry):
        up[p] = dot(x[token_rows(p)], wu[...]).astype(bf16)
        copy_a(p, 0).wait_recv()
        send_b[p, 0, pl.ds(0, half)] = (
            gate[p, own_rows(right, 0, half)] + recv_a[p, 0].astype(f32)
        ).astype(bf16)
        send_b[p, 0, pl.ds(half, half)] = gate[p, own_rows(right, half, half)].astype(bf16)
        copy_b(p, 0).start()
        copy_a(p, 1).wait_recv()
        send_b[p, 1, pl.ds(0, half)] = gate[p, own_rows(left, 0, half)].astype(bf16)
        send_b[p, 1, pl.ds(half, half)] = (
            gate[p, own_rows(left, half, half)] + recv_a[p, 1].astype(f32)
        ).astype(bf16)
        copy_b(p, 1).start()
        hg[p] = dot_nt(og[token_rows(p)], wd[...]).astype(bf16)
        return carry

    lax.fori_loop(0, nq, terms_step, 0)

    for k in range(1, n_col):
        copy_ends(k).wait_recv()
    total = ends_part[...].astype(f32)
    for k in range(1, n_col):
        total += ends_recv[k - 1].astype(f32)
    ends[mine] = total.astype(bf16)

    def copy_gather(k, owner):
        rows = pl.ds(pl.multiple_of((upper_y * n_z + owner) * slab, slab), slab)
        return remote(
            ends.at[rows],
            ends.at[rows],
            gather_s.at[k - 1],
            gather_r.at[k - 1],
            **along_z(k),
        )

    def copy_pair(owner):
        rows = pl.ds(pl.multiple_of(owner * n_z * slab, n_z * slab), n_z * slab)
        return remote(ends.at[rows], ends.at[rows], pair_s, pair_r, **along_y(0, 1))

    for k in range(1, n_z):
        copy_gather(k, z).start()

    loads["store"].wait()
    squares = jnp.zeros((store.shape[0], LANES), f32)
    for j in range(store.shape[1] // LANES):
        value = store[:, pl.ds(j * LANES, LANES)].astype(f32)
        squares += value * value
    upper = squares.astype(bf16)
    lower = (squares - upper.astype(f32)).astype(bf16)
    ones = jnp.ones((8, LANES), bf16)
    doc_squares = dot_nt(ones, upper) + dot_nt(ones, lower)
    loads["mask"].wait()
    keep = jnp.where(c < n_col // 2, mask[0:1, :], mask[1:2, :]).astype(f32)
    doc_squares = doc_squares * keep
    out_width = store.shape[0] // n_col
    for j in range(n_col):
        norm_send[j] = doc_squares[:, j * out_width : (j + 1) * out_width]

    def copy_norm(k):
        to = lax.rem(c + k, n_col)
        return remote(
            norm_send.at[to], norm_recv.at[k - 1], norm_s.at[k - 1], norm_r.at[k - 1], col=to
        )

    def own_step(p, carry):
        copy_b(p, 0).wait_recv()
        copy_b(p, 1).wait_recv()
        value = (
            gate[p, own_rows(c, 0, part)] + recv_b[p, 0].astype(f32) + recv_b[p, 1].astype(f32)
        )
        s[p, c] = (value * jax.nn.sigmoid(value)).astype(bf16)
        copy_g(p, 0, c).start()
        copy_g(p, 1, c).start()
        return carry

    def forward_step(p, carry):
        copy_g(p, 0, left).wait_recv()
        copy_f(p, 0, left).start()
        copy_g(p, 1, right).wait_recv()
        copy_f(p, 1, right).start()
        return carry

    lax.fori_loop(0, early, own_step, 0)
    for k in range(1, n_col):
        copy_norm(k).start()

    n_query = n_grp * nq
    n_sub = x_recv.shape[2]
    for k in range(1, n_z):
        copy_gather(k, lax.rem(z + n_z - k, n_z)).wait_recv()
    copy_pair(upper_y).start()
    lax.fori_loop(0, early - 1, forward_step, 0)
    copy_pair(1 - upper_y).wait_recv()
    low_lanes = lax.broadcasted_iota(jnp.int32, (SEQ, LANES), 1) < k_dim

    def ends_step(p, carry):
        value = ends[token_rows(p)].astype(f32)
        ends_t[p] = value.T[:k_dim].astype(bf16)
        ui2[p] = jnp.where(low_lanes, pltpu.roll(value, k_dim, 1), value).astype(bf16)
        return carry

    lax.fori_loop(0, nq, ends_step, 0)

    lax.fori_loop(early, early + 1, own_step, 0)
    lax.fori_loop(early - 1, early, forward_step, 0)
    lax.fori_loop(early + 1, nq, own_step, 0)

    loads["pdi"].wait()
    loads["pdi2"].wait()
    loads["puo"].wait()
    low_half = lax.broadcasted_iota(jnp.int32, (k_dim // 2, LANES), 1) < k_dim

    def grads_step(p, carry):
        copy_f(p, 0, across).wait_recv()
        copy_f(p, 1, across).wait_recv()
        shared = s[p].reshape(SEQ, s.shape[-1])
        down_in = dot_nt(up[p] * shared, pdi[...])
        up_out = dot_nt(puo[...], hg[p] * shared)
        pairs[pl.ds(0, k_dim)] = dot(ends_t[p], down_in.astype(bf16))
        pairs[pl.ds(k_dim, k_dim)] = dot(up_out.astype(bf16), ui2[p])
        for m in range(2):
            even = pairs[pl.ds(m * k_dim, k_dim // 2, 2)]
            odd = pairs[pl.ds(m * k_dim + 1, k_dim // 2, 2)]
            value = jnp.where(low_half, even, odd)
            grads[p, pl.ds(m * (k_dim // 2), k_dim // 2)] = value
            grads_send[p, pl.ds(m * (k_dim // 2), k_dim // 2)] = value.astype(bf16)
        return carry

    def copy_x(batch, k):
        first, count = batches[batch]
        to = lax.rem(c + k, n_col)
        return remote(
            grads_send.at[
                pl.ds(first, count), pl.ds(pl.multiple_of(to * n_sub, n_sub), n_sub)
            ],
            x_recv.at[k - 1, pl.ds(first, count)],
            x_s.at[batch, k - 1],
            x_r.at[batch, k - 1],
            col=to,
        )

    def copy_z(batch, k):
        first, count = batches[batch]
        return remote(
            block_send.at[pl.ds(first, count)],
            z_recv.at[k - 1, pl.ds(first, count)],
            z_s.at[batch, k - 1],
            z_r.at[batch, k - 1],
            **along_z(k),
        )

    def copy_y(batch, j, e):
        first, count = batches[batch]
        return remote(
            y_send.at[pl.ds(first, count)],
            y_recv.at[j, e, pl.ds(first, count)],
            y_s.at[batch, j, e],
            y_r.at[batch, j, e],
            **along_y(j, e),
        )

    def make_grads(batch):
        first, count = batches[batch]
        lax.fori_loop(first, first + count, grads_step, 0)
        for k in x_steps:
            copy_x(batch, k).start()

    def sum_col(batch):
        first, count = batches[batch]
        span = pl.ds(first, count)
        for k in range(1, n_col):
            copy_x(batch, k).wait_recv()
        total = grads[span, pl.ds(pl.multiple_of(c * n_sub, n_sub), n_sub)]
        for k in range(1, n_col):
            total += x_recv[k - 1, span].astype(f32)
        block[span] = total
        block_send[span] = total.astype(bf16)

        for k in z_steps:
            copy_z(batch, k).start()

    def sum_z(batch):
        first, count = batches[batch]
        span = pl.ds(first, count)

        for k in range(1, n_z):
            copy_z(batch, k).wait_recv()
        total = block[span]
        for k in range(1, n_z):
            total += z_recv[k - 1, span].astype(f32)
        block[span] = total
        y_send[span] = total.astype(bf16)
        for j, e in y_steps:
            copy_y(batch, j, e).start()

    def sum_y(batch):
        first, count = batches[batch]
        span = pl.ds(first, count)
        for j in range(n_grp):
            copy_y(batch, j, 1).wait_recv()
            if j:
                copy_y(batch, j, 0).wait_recv()
                total = y_recv[j, 0, span].astype(f32)
            else:
                total = block[span]
            total += y_recv[j, 1, span].astype(f32)
            for q in range(count):
                row = lax.rem(g + n_grp - j, n_grp) * nq + first + q
                full[pl.ds(row, n_sub, n_query), :] = total[q]

    make_grads(0)
    lax.fori_loop(early, nq, forward_step, 0)
    sum_col(0)
    make_grads(1)
    make_grads(2)
    sum_col(1)
    sum_z(0)
    sum_col(2)
    sum_z(1)
    sum_y(0)
    sum_z(2)
    sum_y(1)
    sum_y(2)

    query = jnp.concatenate(
        [full[pl.ds(kk * n_query, n_query), :] for kk in range(n_sub)], axis=1
    )
    raw = dot_nt(query.astype(bf16), store[...]) * keep
    query_squares = jnp.broadcast_to(
        jnp.sum(query * query, axis=1, keepdims=True), (n_query, out_width)
    )
    for j in range(n_col):
        c_send[j] = jnp.concatenate(
            [raw[:, j * out_width : (j + 1) * out_width], query_squares], axis=0
        ).astype(bf16)

    def copy_c(k):
        to = lax.rem(c + k, n_col)
        return remote(c_send.at[to], c_recv.at[k - 1], c_s.at[k - 1], c_r.at[k - 1], col=to)

    for k in x_steps:
        copy_c(k).start()
    def ring_done(p, carry):
        for way in range(2):
            copy_a(p, way).wait_send()
            copy_b(p, way).wait_send()
            copy_g(p, way, c).wait_send()
            copy_f(p, way, left).wait_send()
        return carry

    lax.fori_loop(0, nq, ring_done, 0)

    for k in range(1, n_z):
        copy_gather(k, z).wait_send()
        for batch in range(len(batches)):
            copy_z(batch, k).wait_send()
    copy_pair(upper_y).wait_send()
    for k in range(1, n_col):
        copy_ends(k).wait_send()
        copy_norm(k).wait_send()
        for batch in range(len(batches)):
            copy_x(batch, k).wait_send()
    for j, e in y_steps:
        for batch in range(len(batches)):
            copy_y(batch, j, e).wait_send()
    norms = norm_send[c]
    for k in range(1, n_col):
        copy_norm(k).wait_recv()
        norms += norm_recv[k - 1]
    columns = float(n_col * n_sub * LANES)
    doc_norm = jnp.sqrt(norms[0:1] / columns + EPSILON) * math.sqrt(columns)
    total = c_send[c].astype(f32)
    for k in range(1, n_col):
        copy_c(k).wait_recv()
    for k in range(1, n_col):
        total += c_recv[k - 1].astype(f32)
    query_norm = jnp.sqrt(total[n_query:] / columns + EPSILON)
    scores = total[:n_query] / (query_norm * doc_norm)
    slot = c * out_width + lax.broadcasted_iota(jnp.int32, scores.shape, 1)
    loads["live"].wait()
    out_ref[...] = jnp.where(slot < live[0], scores, 0.0)
    for k in x_steps:
        copy_c(k).wait_send()


def local(
    mlp_input,
    out_grad,
    w_gate,
    w_up,
    w_down,
    proj_down_in,
    proj_down_out,
    proj_up_in,
    proj_up_out,
    store,
    layer_mask,
    live_count,
):
    n_grp, n_doc, n_col = (lax.axis_size(name) for name in ("grp", "doc", "col"))
    tokens, depth = mlp_input.shape
    width = w_gate.shape[1]
    k_dim = proj_down_in.shape[1]
    nq = tokens // SEQ
    part = SEQ // n_col
    slab = tokens // n_doc
    n_row = 2 * k_dim * k_dim // LANES
    n_sub = n_row // n_col
    out_width = store.shape[0] // n_col
    dma = pltpu.SemaphoreType.DMA
    scratch = [
        pltpu.VMEM((tokens, depth), bf16),
        pltpu.VMEM((tokens, depth), bf16),
        pltpu.VMEM((depth, width), bf16),
        pltpu.VMEM((depth, width), bf16),
        pltpu.VMEM((width, depth), bf16),
        pltpu.VMEM((2 * k_dim, width), bf16),
        pltpu.VMEM((2 * k_dim, depth), bf16),
        pltpu.VMEM((2 * k_dim, depth), bf16),
        pltpu.VMEM((k_dim, width), bf16),
        pltpu.VMEM(store.shape, bf16),
        pltpu.VMEM(layer_mask.shape[::-1], jnp.int32),
        pltpu.SMEM(live_count.shape, jnp.int32),
        pltpu.VMEM((nq, SEQ, width), f32),
        pltpu.VMEM((nq, SEQ, width), bf16),
        pltpu.VMEM((nq, SEQ, width), bf16),
        pltpu.VMEM((nq, n_col, part, width), bf16),
        pltpu.VMEM((nq, part, width), bf16),
        pltpu.VMEM((nq, 2, part // 2, width), bf16),
        pltpu.VMEM((nq, 2, part, width), bf16),
        pltpu.VMEM((nq, 2, part, width), bf16),
        pltpu.VMEM((slab, LANES), bf16),
        pltpu.VMEM((n_col - 1, slab, LANES), bf16),
        pltpu.VMEM((tokens, LANES), bf16),
        pltpu.VMEM((nq, k_dim, SEQ), bf16),
        pltpu.VMEM((nq, SEQ, LANES), bf16),
        pltpu.VMEM((2 * k_dim + 8, LANES), f32),
        pltpu.VMEM((nq, n_row, LANES), f32),
        pltpu.VMEM((nq, n_row, LANES), bf16),
        pltpu.VMEM((n_col - 1, nq, n_sub, LANES), bf16),
        pltpu.VMEM((nq, n_sub, LANES), f32),
        pltpu.VMEM((nq, n_sub, LANES), bf16),
        pltpu.VMEM((n_doc // 2 - 1, nq, n_sub, LANES), bf16),
        pltpu.VMEM((nq, n_sub, LANES), bf16),
        pltpu.VMEM((n_grp, 2, nq, n_sub, LANES), bf16),
        pltpu.VMEM(((n_sub + 1) * n_grp * nq, LANES), f32),
        pltpu.VMEM((n_col, 8, out_width), f32),
        pltpu.VMEM((n_col - 1, 8, out_width), f32),
        pltpu.VMEM((n_col, 2 * n_grp * nq, out_width), bf16),
        pltpu.VMEM((n_col - 1, 2 * n_grp * nq, out_width), bf16),
        dma((12,)),
        dma((nq,)),
        dma((4, nq, 2)),
        dma((4, nq, 2)),
        dma((n_col - 1,)),
        dma((n_col - 1,)),
        dma((n_doc // 2 - 1,)),
        dma((n_doc // 2 - 1,)),
        dma(()),
        dma(()),
        dma((3, n_col - 1)),
        dma((3, n_col - 1)),
        dma((3, n_doc // 2 - 1)),
        dma((3, n_doc // 2 - 1)),
        dma((3, n_grp, 2)),
        dma((3, n_grp, 2)),
        dma((n_col - 1,)),
        dma((n_col - 1,)),
        dma((n_col - 1,)),
        dma((n_col - 1,)),
    ]
    scores = pl.pallas_call(
        functools.partial(kernel, (n_grp, n_doc, n_col, nq)),
        out_shape=jax.ShapeDtypeStruct((n_grp * nq, out_width), f32),
        in_specs=[pl.BlockSpec(memory_space=pl.ANY)] * 12,
        out_specs=pl.BlockSpec(memory_space=pltpu.VMEM),
        scratch_shapes=scratch,
        compiler_params=pltpu.CompilerParams(
            collective_id=0, has_side_effects=True, vmem_limit_bytes=58 * 1024 * 1024
        ),
        cost_estimate=pl.CostEstimate(
            flops=6 * tokens * depth * width, bytes_accessed=14 << 20, transcendentals=0
        ),
    )(
        mlp_input,
        out_grad,
        w_gate,
        w_up,
        w_down,
        proj_down_in.T,
        proj_down_out.T,
        proj_up_in.T,
        proj_up_out.T,
        store,
        layer_mask.T,
        live_count,
    )
    return scores


def solution(mesh):
    return jax.shard_map(
        local,
        mesh=mesh,
        in_specs=(
            P("grp", "col"),
            P("grp", "col"),
            P("col", "doc"),
            P("col", "doc"),
            P("doc", "col"),
            P("doc", None),
            P("col", None),
            P("col", None),
            P("doc", None),
            P(("grp", "doc"), "col"),
            P(("grp", "doc"), None),
            P(("grp", "doc")),
        ),
        out_specs=P(None, ("grp", "doc", "col")),
        check_vma=False,
    )
```

```python
import functools
import math

import jax
import jax.numpy as jnp
from jax import lax
from jax.experimental import pallas as pl
from jax.experimental.pallas import tpu as pltpu
from jax.sharding import PartitionSpec as P

MESH = pl.DeviceIdType.MESH
SEQ = 256
LANES = 128
EPSILON = 1e-06
NT = (((1,), (1,)), ((), ()))
f32, bf16 = jnp.float32, jnp.bfloat16


def dot(left, right):
    return jnp.dot(left, right, preferred_element_type=f32)


def dot_nt(left, right):
    return lax.dot_general(left, right, NT, preferred_element_type=f32)


def kernel(
    sizes,
    x_in,
    og_in,
    wg_in,
    wu_in,
    wd_in,
    pdi_in,
    pdo_in,
    pui_in,
    puo_in,
    store_in,
    mask_in,
    live_in,
    out_ref,
    x,
    og,
    wg,
    wu,
    wd,
    pdi,
    pdo,
    pui,
    puo,
    store,
    mask,
    live,
    gate,
    up,
    hg,
    s,
    send_a,
    recv_a,
    send_b,
    recv_b,
    ends_part,
    ends_recv,
    ends,
    ends_t,
    ui2,
    pairs,
    grads,
    grads_send,
    x_recv,
    block,
    block_send,
    z_recv,
    y_send,
    y_recv,
    full,
    norm_send,
    norm_recv,
    c_send,
    c_recv,
    load_sem,
    x_load_sem,
    ring_s,
    ring_r,
    ends_s,
    ends_r,
    gather_s,
    gather_r,
    pair_s,
    pair_r,
    x_s,
    x_r,
    z_s,
    z_r,
    y_s,
    y_r,
    norm_s,
    norm_r,
    c_s,
    c_r,
):
    n_grp, n_doc, n_col, nq = sizes
    part = SEQ // n_col
    half = part // 2
    early = nq // 2
    batches = ((0, early), (early, nq - 1 - early), (nq - 1, 1))
    g, d, c = lax.axis_index("grp"), lax.axis_index("doc"), lax.axis_index("col")
    right, left, across = (
        lax.rem(c + 1, n_col),
        lax.rem(c + n_col - 1, n_col),
        lax.rem(c + 2, n_col),
    )
    n_z = n_doc // 2
    z, upper_y = d // 2, lax.rem(d, 2)
    k_dim = pdi_in.shape[0]

    def along_z(k):
        return {"doc": lax.rem(z + k, n_z) * 2 + upper_y}

    def along_y(j, e):
        return {"grp": lax.rem(g + j, n_grp), "doc": z * 2 + (upper_y + e - 2 * upper_y * e)}

    x_steps = sorted(range(1, n_col), key=lambda k: -min(k, n_col - k))
    z_steps = sorted(range(1, n_z), key=lambda k: -min(k, n_z - k))
    y_steps = [(j, e) for e in (1, 0) for j in range(n_grp) if j or e]

    def remote(src, dst, send, recv, **place):
        return pltpu.make_async_remote_copy(
            src_ref=src,
            dst_ref=dst,
            send_sem=send,
            recv_sem=recv,
            device_id=place,
            device_id_type=MESH,
        )

    def token_rows(p):
        return pl.ds(pl.multiple_of(p * SEQ, SEQ), SEQ)

    def own_rows(owner, first, count):
        return pl.ds(pl.multiple_of(owner * part + first, half), count)

    loads = {}

    def load(key, src, dst):
        copy = pltpu.make_async_copy(src, dst, load_sem.at[len(loads)])
        copy.start()
        loads[key] = copy

    def x_load(p):
        return pltpu.make_async_copy(
            x_in.at[token_rows(p)], x.at[token_rows(p)], x_load_sem.at[p]
        )

    load("wg", wg_in, wg)
    x_load(0).start()

    barrier = pltpu.get_barrier_semaphore()

    def greet(place):
        pl.semaphore_signal(barrier, 1, device_id=place, device_id_type=MESH)

    for k in z_steps:
        greet(along_z(k))
    for j, e in y_steps:
        greet(along_y(j, e))
    for k in x_steps:
        greet({"col": lax.rem(c + k, n_col)})
    for p in range(1, nq):
        x_load(p).start()

    loads["wg"].wait()
    x_load(0).wait()
    load("og", og_in, og)
    load("pdo", pdo_in, pdo.at[pl.ds(0, k_dim)])
    load("pui", pui_in, pui.at[pl.ds(k_dim, k_dim)])
    load("wu", wu_in, wu)
    load("wd", wd_in, wd)
    load("store", store_in, store)
    load("mask", mask_in, mask)
    load("pdi", pdi_in, pdi.at[pl.ds(0, k_dim)])
    load("pdi2", pdi_in, pdi.at[pl.ds(k_dim, k_dim)])
    load("puo", puo_in, puo)
    load("live", live_in, live)

    def gate_term(p):
        gate[p] = dot(x[token_rows(p)], wg[...])
        send_a[p] = gate[p, own_rows(across, 0, part)].astype(bf16)

    first_rows = pl.ds(pl.multiple_of(across * part, part), part)
    send_a[0] = dot(x[first_rows], wg[...]).astype(bf16)
    pl.semaphore_wait(barrier, n_z - 1 + len(y_steps) + n_col - 1)

    def copy_a(p, way):
        rows = pl.ds(way * half, half)
        return remote(
            send_a.at[p, rows],
            recv_a.at[p, way],
            ring_s.at[0, p, way],
            ring_r.at[0, p, way],
            col=(right, left)[way],
        )

    def copy_b(p, way):
        return remote(
            send_b.at[p, way],
            recv_b.at[p, way],
            ring_s.at[1, p, way],
            ring_r.at[1, p, way],
            col=(right, left)[way],
        )

    def copy_g(p, way, slot):
        return remote(
            s.at[p, slot],
            s.at[p, slot],
            ring_s.at[2, p, way],
            ring_r.at[2, p, way],
            col=(right, left)[way],
        )

    def copy_f(p, way, slot):
        rows = pl.ds(way * half, half)
        return remote(
            s.at[p, slot, rows],
            s.at[p, slot, rows],
            ring_s.at[3, p, way],
            ring_r.at[3, p, way],
            col=(right, left)[way],
        )

    copy_a(0, 0).start()
    copy_a(0, 1).start()

    def gate_step(p, carry):
        x_load(p).wait()
        gate_term(p)
        copy_a(p, 0).start()
        copy_a(p, 1).start()
        return carry

    lax.fori_loop(1, nq, gate_step, 0)
    gate[0] = dot(x[token_rows(0)], wg[...])

    slab = ends_part.shape[0]
    loads["og"].wait()
    loads["pdo"].wait()
    loads["pui"].wait()
    pdo[pl.ds(k_dim, k_dim)] = jnp.zeros((k_dim, pdo.shape[1]), bf16)
    pui[pl.ds(0, k_dim)] = jnp.zeros((k_dim, pui.shape[1]), bf16)
    mine = pl.ds(pl.multiple_of((upper_y * n_z + z) * slab, slab), slab)
    ends_part[...] = (dot_nt(og[mine], pdo[...]) + dot_nt(x[mine], pui[...])).astype(bf16)

    def copy_ends(k):
        return remote(
            ends_part,
            ends_recv.at[k - 1],
            ends_s.at[k - 1],
            ends_r.at[k - 1],
            col=lax.rem(c + k, n_col),
        )

    for k in range(1, n_col):
        copy_ends(k).start()

    loads["wu"].wait()
    loads["wd"].wait()

    def terms_step(p, carry):
        up[p] = dot(x[token_rows(p)], wu[...]).astype(bf16)
        copy_a(p, 0).wait_recv()
        send_b[p, 0, pl.ds(0, half)] = (
            gate[p, own_rows(right, 0, half)] + recv_a[p, 0].astype(f32)
        ).astype(bf16)
        send_b[p, 0, pl.ds(half, half)] = gate[p, own_rows(right, half, half)].astype(bf16)
        copy_b(p, 0).start()
        copy_a(p, 1).wait_recv()
        send_b[p, 1, pl.ds(0, half)] = gate[p, own_rows(left, 0, half)].astype(bf16)
        send_b[p, 1, pl.ds(half, half)] = (
            gate[p, own_rows(left, half, half)] + recv_a[p, 1].astype(f32)
        ).astype(bf16)
        copy_b(p, 1).start()
        hg[p] = dot_nt(og[token_rows(p)], wd[...]).astype(bf16)
        return carry

    lax.fori_loop(0, nq, terms_step, 0)

    for k in range(1, n_col):
        copy_ends(k).wait_recv()
    total = ends_part[...].astype(f32)
    for k in range(1, n_col):
        total += ends_recv[k - 1].astype(f32)
    ends[mine] = total.astype(bf16)

    def copy_gather(k, owner):
        rows = pl.ds(pl.multiple_of((upper_y * n_z + owner) * slab, slab), slab)
        return remote(
            ends.at[rows],
            ends.at[rows],
            gather_s.at[k - 1],
            gather_r.at[k - 1],
            **along_z(k),
        )

    def copy_pair(owner):
        rows = pl.ds(pl.multiple_of(owner * n_z * slab, n_z * slab), n_z * slab)
        return remote(ends.at[rows], ends.at[rows], pair_s, pair_r, **along_y(0, 1))

    for k in range(1, n_z):
        copy_gather(k, z).start()

    loads["store"].wait()
    squares = jnp.zeros((store.shape[0], LANES), f32)
    for j in range(store.shape[1] // LANES):
        value = store[:, pl.ds(j * LANES, LANES)].astype(f32)
        squares += value * value
    upper = squares.astype(bf16)
    lower = (squares - upper.astype(f32)).astype(bf16)
    ones = jnp.ones((8, LANES), bf16)
    doc_squares = dot_nt(ones, upper) + dot_nt(ones, lower)
    loads["mask"].wait()
    keep = jnp.where(c < n_col // 2, mask[0:1, :], mask[1:2, :]).astype(f32)
    doc_squares = doc_squares * keep
    out_width = store.shape[0] // n_col
    for j in range(n_col):
        norm_send[j] = doc_squares[:, j * out_width : (j + 1) * out_width]

    def copy_norm(k):
        to = lax.rem(c + k, n_col)
        return remote(
            norm_send.at[to], norm_recv.at[k - 1], norm_s.at[k - 1], norm_r.at[k - 1], col=to
        )

    def own_step(p, carry):
        copy_b(p, 0).wait_recv()
        copy_b(p, 1).wait_recv()
        value = (
            gate[p, own_rows(c, 0, part)] + recv_b[p, 0].astype(f32) + recv_b[p, 1].astype(f32)
        )
        s[p, c] = (value * jax.nn.sigmoid(value)).astype(bf16)
        copy_g(p, 0, c).start()
        copy_g(p, 1, c).start()
        return carry

    def forward_step(p, carry):
        copy_g(p, 0, left).wait_recv()
        copy_f(p, 0, left).start()
        copy_g(p, 1, right).wait_recv()
        copy_f(p, 1, right).start()
        return carry

    lax.fori_loop(0, early, own_step, 0)
    for k in range(1, n_col):
        copy_norm(k).start()

    n_query = n_grp * nq
    n_sub = x_recv.shape[2]
    for k in range(1, n_z):
        copy_gather(k, lax.rem(z + n_z - k, n_z)).wait_recv()
    copy_pair(upper_y).start()
    lax.fori_loop(0, early - 1, forward_step, 0)
    copy_pair(1 - upper_y).wait_recv()
    low_lanes = lax.broadcasted_iota(jnp.int32, (SEQ, LANES), 1) < k_dim

    def ends_step(p, carry):
        value = ends[token_rows(p)].astype(f32)
        ends_t[p] = value.T[:k_dim].astype(bf16)
        ui2[p] = jnp.where(low_lanes, pltpu.roll(value, k_dim, 1), value).astype(bf16)
        return carry

    lax.fori_loop(0, nq, ends_step, 0)

    lax.fori_loop(early, early + 1, own_step, 0)
    lax.fori_loop(early - 1, early, forward_step, 0)
    lax.fori_loop(early + 1, nq, own_step, 0)

    loads["pdi"].wait()
    loads["pdi2"].wait()
    loads["puo"].wait()
    low_half = lax.broadcasted_iota(jnp.int32, (k_dim // 2, LANES), 1) < k_dim

    def grads_step(p, carry):
        copy_f(p, 0, across).wait_recv()
        copy_f(p, 1, across).wait_recv()
        shared = s[p].reshape(SEQ, s.shape[-1])
        down_in = dot_nt(up[p] * shared, pdi[...])
        up_out = dot_nt(puo[...], hg[p] * shared)
        pairs[pl.ds(0, k_dim)] = dot(ends_t[p], down_in.astype(bf16))
        pairs[pl.ds(k_dim, k_dim)] = dot(up_out.astype(bf16), ui2[p])
        for m in range(2):
            even = pairs[pl.ds(m * k_dim, k_dim // 2, 2)]
            odd = pairs[pl.ds(m * k_dim + 1, k_dim // 2, 2)]
            value = jnp.where(low_half, even, odd)
            grads[p, pl.ds(m * (k_dim // 2), k_dim // 2)] = value
            grads_send[p, pl.ds(m * (k_dim // 2), k_dim // 2)] = value.astype(bf16)
        return carry

    def copy_x(batch, k):
        first, count = batches[batch]
        to = lax.rem(c + k, n_col)
        return remote(
            grads_send.at[
                pl.ds(first, count), pl.ds(pl.multiple_of(to * n_sub, n_sub), n_sub)
            ],
            x_recv.at[k - 1, pl.ds(first, count)],
            x_s.at[batch, k - 1],
            x_r.at[batch, k - 1],
            col=to,
        )

    def copy_z(batch, k):
        first, count = batches[batch]
        return remote(
            block_send.at[pl.ds(first, count)],
            z_recv.at[k - 1, pl.ds(first, count)],
            z_s.at[batch, k - 1],
            z_r.at[batch, k - 1],
            **along_z(k),
        )

    def copy_y(batch, j, e):
        first, count = batches[batch]
        return remote(
            y_send.at[pl.ds(first, count)],
            y_recv.at[j, e, pl.ds(first, count)],
            y_s.at[batch, j, e],
            y_r.at[batch, j, e],
            **along_y(j, e),
        )

    def make_grads(batch):
        first, count = batches[batch]
        lax.fori_loop(first, first + count, grads_step, 0)
        for k in x_steps:
            copy_x(batch, k).start()

    def sum_col(batch):
        first, count = batches[batch]
        span = pl.ds(first, count)
        for k in range(1, n_col):
            copy_x(batch, k).wait_recv()
        total = grads[span, pl.ds(pl.multiple_of(c * n_sub, n_sub), n_sub)]
        for k in range(1, n_col):
            total += x_recv[k - 1, span].astype(f32)
        block[span] = total
        block_send[span] = total.astype(bf16)

        for k in z_steps:
            copy_z(batch, k).start()

    def sum_z(batch):
        first, count = batches[batch]
        span = pl.ds(first, count)

        for k in range(1, n_z):
            copy_z(batch, k).wait_recv()
        total = block[span]
        for k in range(1, n_z):
            total += z_recv[k - 1, span].astype(f32)
        block[span] = total
        y_send[span] = total.astype(bf16)
        for j, e in y_steps:
            copy_y(batch, j, e).start()

    def sum_y(batch):
        first, count = batches[batch]
        span = pl.ds(first, count)
        for j in range(n_grp):
            copy_y(batch, j, 1).wait_recv()
            if j:
                copy_y(batch, j, 0).wait_recv()
                total = y_recv[j, 0, span].astype(f32)
            else:
                total = block[span]
            total += y_recv[j, 1, span].astype(f32)
            for q in range(count):
                row = lax.rem(g + n_grp - j, n_grp) * nq + first + q
                full[pl.ds(row, n_sub, n_query), :] = total[q]

    make_grads(0)
    lax.fori_loop(early, nq, forward_step, 0)
    sum_col(0)
    make_grads(1)
    make_grads(2)
    sum_col(1)
    sum_z(0)
    sum_col(2)
    sum_z(1)
    sum_y(0)
    sum_z(2)
    sum_y(1)
    sum_y(2)

    query = jnp.concatenate(
        [full[pl.ds(kk * n_query, n_query), :] for kk in range(n_sub)], axis=1
    )
    query_squares = jnp.broadcast_to(
        jnp.sum(query * query, axis=1, keepdims=True), (n_query, out_width)
    )
    query = query.astype(bf16)

    def scores_for(owner):
        docs = pl.ds(pl.multiple_of(owner * out_width, out_width), out_width)
        kept = jnp.where(c < n_col // 2, mask[0:1, docs], mask[1:2, docs]).astype(f32)
        raw = dot_nt(query, store[docs, :]) * kept
        return jnp.concatenate([raw, query_squares], axis=0).astype(bf16)

    def copy_c(k):
        to = lax.rem(c + k, n_col)
        return remote(c_send.at[to], c_recv.at[k - 1], c_s.at[k - 1], c_r.at[k - 1], col=to)

    for k in x_steps:
        c_send[lax.rem(c + k, n_col)] = scores_for(lax.rem(c + k, n_col))
        copy_c(k).start()
    total = scores_for(c).astype(f32)
    def ring_done(p, carry):
        for way in range(2):
            copy_a(p, way).wait_send()
            copy_b(p, way).wait_send()
            copy_g(p, way, c).wait_send()
            copy_f(p, way, left).wait_send()
        return carry

    lax.fori_loop(0, nq, ring_done, 0)

    for k in range(1, n_z):
        copy_gather(k, z).wait_send()
        for batch in range(len(batches)):
            copy_z(batch, k).wait_send()
    copy_pair(upper_y).wait_send()
    for k in range(1, n_col):
        copy_ends(k).wait_send()
        copy_norm(k).wait_send()
        for batch in range(len(batches)):
            copy_x(batch, k).wait_send()
    for j, e in y_steps:
        for batch in range(len(batches)):
            copy_y(batch, j, e).wait_send()
    norms = norm_send[c]
    for k in range(1, n_col):
        copy_norm(k).wait_recv()
        norms += norm_recv[k - 1]
    columns = float(n_col * n_sub * LANES)
    doc_norm = jnp.sqrt(norms[0:1] / columns + EPSILON) * math.sqrt(columns)
    for k in range(1, n_col):
        copy_c(k).wait_recv()
    for k in range(1, n_col):
        total += c_recv[k - 1].astype(f32)
    query_norm = jnp.sqrt(total[n_query:] / columns + EPSILON)
    scores = total[:n_query] / (query_norm * doc_norm)
    slot = c * out_width + lax.broadcasted_iota(jnp.int32, scores.shape, 1)
    loads["live"].wait()
    out_ref[...] = jnp.where(slot < live[0], scores, 0.0)
    for k in x_steps:
        copy_c(k).wait_send()


def local(
    mlp_input,
    out_grad,
    w_gate,
    w_up,
    w_down,
    proj_down_in,
    proj_down_out,
    proj_up_in,
    proj_up_out,
    store,
    layer_mask,
    live_count,
):
    n_grp, n_doc, n_col = (lax.axis_size(name) for name in ("grp", "doc", "col"))
    tokens, depth = mlp_input.shape
    width = w_gate.shape[1]
    k_dim = proj_down_in.shape[1]
    nq = tokens // SEQ
    part = SEQ // n_col
    slab = tokens // n_doc
    n_row = 2 * k_dim * k_dim // LANES
    n_sub = n_row // n_col
    out_width = store.shape[0] // n_col
    dma = pltpu.SemaphoreType.DMA
    scratch = [
        pltpu.VMEM((tokens, depth), bf16),
        pltpu.VMEM((tokens, depth), bf16),
        pltpu.VMEM((depth, width), bf16),
        pltpu.VMEM((depth, width), bf16),
        pltpu.VMEM((width, depth), bf16),
        pltpu.VMEM((2 * k_dim, width), bf16),
        pltpu.VMEM((2 * k_dim, depth), bf16),
        pltpu.VMEM((2 * k_dim, depth), bf16),
        pltpu.VMEM((k_dim, width), bf16),
        pltpu.VMEM(store.shape, bf16),
        pltpu.VMEM(layer_mask.shape[::-1], jnp.int32),
        pltpu.SMEM(live_count.shape, jnp.int32),
        pltpu.VMEM((nq, SEQ, width), f32),
        pltpu.VMEM((nq, SEQ, width), bf16),
        pltpu.VMEM((nq, SEQ, width), bf16),
        pltpu.VMEM((nq, n_col, part, width), bf16),
        pltpu.VMEM((nq, part, width), bf16),
        pltpu.VMEM((nq, 2, part // 2, width), bf16),
        pltpu.VMEM((nq, 2, part, width), bf16),
        pltpu.VMEM((nq, 2, part, width), bf16),
        pltpu.VMEM((slab, LANES), bf16),
        pltpu.VMEM((n_col - 1, slab, LANES), bf16),
        pltpu.VMEM((tokens, LANES), bf16),
        pltpu.VMEM((nq, k_dim, SEQ), bf16),
        pltpu.VMEM((nq, SEQ, LANES), bf16),
        pltpu.VMEM((2 * k_dim + 8, LANES), f32),
        pltpu.VMEM((nq, n_row, LANES), f32),
        pltpu.VMEM((nq, n_row, LANES), bf16),
        pltpu.VMEM((n_col - 1, nq, n_sub, LANES), bf16),
        pltpu.VMEM((nq, n_sub, LANES), f32),
        pltpu.VMEM((nq, n_sub, LANES), bf16),
        pltpu.VMEM((n_doc // 2 - 1, nq, n_sub, LANES), bf16),
        pltpu.VMEM((nq, n_sub, LANES), bf16),
        pltpu.VMEM((n_grp, 2, nq, n_sub, LANES), bf16),
        pltpu.VMEM(((n_sub + 1) * n_grp * nq, LANES), f32),
        pltpu.VMEM((n_col, 8, out_width), f32),
        pltpu.VMEM((n_col - 1, 8, out_width), f32),
        pltpu.VMEM((n_col, 2 * n_grp * nq, out_width), bf16),
        pltpu.VMEM((n_col - 1, 2 * n_grp * nq, out_width), bf16),
        dma((12,)),
        dma((nq,)),
        dma((4, nq, 2)),
        dma((4, nq, 2)),
        dma((n_col - 1,)),
        dma((n_col - 1,)),
        dma((n_doc // 2 - 1,)),
        dma((n_doc // 2 - 1,)),
        dma(()),
        dma(()),
        dma((3, n_col - 1)),
        dma((3, n_col - 1)),
        dma((3, n_doc // 2 - 1)),
        dma((3, n_doc // 2 - 1)),
        dma((3, n_grp, 2)),
        dma((3, n_grp, 2)),
        dma((n_col - 1,)),
        dma((n_col - 1,)),
        dma((n_col - 1,)),
        dma((n_col - 1,)),
    ]
    scores = pl.pallas_call(
        functools.partial(kernel, (n_grp, n_doc, n_col, nq)),
        out_shape=jax.ShapeDtypeStruct((n_grp * nq, out_width), f32),
        in_specs=[pl.BlockSpec(memory_space=pl.ANY)] * 12,
        out_specs=pl.BlockSpec(memory_space=pltpu.VMEM),
        scratch_shapes=scratch,
        compiler_params=pltpu.CompilerParams(
            collective_id=0, has_side_effects=True, vmem_limit_bytes=58 * 1024 * 1024
        ),
        cost_estimate=pl.CostEstimate(
            flops=6 * tokens * depth * width, bytes_accessed=14 << 20, transcendentals=0
        ),
    )(
        mlp_input,
        out_grad,
        w_gate,
        w_up,
        w_down,
        proj_down_in.T,
        proj_down_out.T,
        proj_up_in.T,
        proj_up_out.T,
        store,
        layer_mask.T,
        live_count,
    )
    return scores


def solution(mesh):
    return jax.shard_map(
        local,
        mesh=mesh,
        in_specs=(
            P("grp", "col"),
            P("grp", "col"),
            P("col", "doc"),
            P("col", "doc"),
            P("doc", "col"),
            P("doc", None),
            P("col", None),
            P("col", None),
            P("doc", None),
            P(("grp", "doc"), "col"),
            P(("grp", "doc"), None),
            P(("grp", "doc")),
        ),
        out_specs=P(None, ("grp", "doc", "col")),
        check_vma=False,
    )
```
